32 devices in a mesh: gz: 8 (over y, x, core), gy: 4 (over z).
Axes of the slice: x: 2, y: 2, z: 4, core: 2. Of those that a mesh axis runs over, the one named last changes fastest.
Arguments:
- init: float32 [128, 512, 512], P('gz', None, 'gy'), may hold values from -6 to 6
- measured: float32 [4, 128, 512, 512], P(None, None, 'gz', 'gy'), may hold values from -70 to 70
- mask: int32 [8, 8], replicated, may hold values from 0 to 1, as said below
- kernel_index: int32 [4, 8, 8], replicated, may hold values from 0 to 15
- kernels: float32 [16, 31], replicated, may hold values from 0.02 to 0.3
Outputs:
- solved: float32 [128, 512, 512], P('gz', None, 'gy')
The draws below stay inside these ranges and needn't reach their ends.
Inputs may be any that keep to these rules, and one draw needn't show every extreme that they name: `mask`: 1 marks a tissue block; in each aligned region of 64 x 128 lateral cells, whose blocks start at multiples of 64 and 128, exactly 1 block is 1.
All inputs are finite; a program needn't handle non-finite values.
Results may differ from the reference program's by a relative error of at most 0.0003.
Values sent between devices are 32-bit elements; how exact they have to be, the bound alone decides.
No kernel may reach another device: no remote copies, remote signals or barrier semaphores. Data moves between devices by JAX's collectives and lax.ppermute only.
A program may use at most 128 MiB of HBM per device.

```python
import math
import jax
import jax.numpy as jnp
from jax import lax

NZ = 128
XT = 64
YD = 128
BX = 64
BY = 64
TISSUE = 1
ZBW = 16
TAPS = 31
VIEWS = 4
NK = 16
ITERS = 4
HALF = 15
ZBANDS = 8
NX = 512
NY = 512
XBLOCKS = 8


def draw_measured(key, part):
    across = jnp.arange(NX, dtype=jnp.float32) / NX
    view_rates = 1.0 + jnp.arange(VIEWS, dtype=jnp.float32) / (VIEWS - 1.0)
    exponent = 0.5 * view_rates[:, None] * across[None, :]
    shape_full = (VIEWS, NZ, NX, NY)
    scale = 10.0 ** exponent
    base = jax.random.truncated_normal(key, -6.0, 6.0, shape_full, jnp.float32)
    return base * scale[:, None, :, None]


def draw_mask(key, part):
    tile_count = NX // XT
    groups = NY // YD
    across = XT // BX
    downward = YD // BY
    region_keys = jax.random.split(key, tile_count * groups)

    def one_region(region_key):
        return jax.random.permutation(region_key, across * downward)
    positions = jax.vmap(one_region)(region_keys)
    tissue_flags = (positions < TISSUE).astype(jnp.int32)
    tissue_flags = tissue_flags.reshape(tile_count, groups, across, downward).transpose(0, 2, 1, 3)
    return tissue_flags.reshape(tile_count * across, groups * downward)


def with_ends(result, stream_key, smallest, top_value):
    extent = result.shape
    index_at = [jax.random.randint(jax.random.fold_in(stream_key, axis), (), 0, extent[axis]) for axis in range(len(extent))]
    result = result.at[tuple(index_at)].set(smallest)
    longest = extent.index(max(extent))
    index_at[longest] = (index_at[longest] + 1) % extent[longest]
    return result.at[tuple(index_at)].set(top_value)


def levels(rng, extent, shards, smallest, largest):
    def one(axis_at, blocks):
        heights = jax.random.uniform(jax.random.fold_in(jax.random.fold_in(rng, 6), axis_at), (blocks,), jnp.float32, smallest / len(shards), largest / len(shards))
        return jnp.repeat(jnp.exp(heights), extent[axis_at] // blocks).reshape((-1,) + (1,) * (len(extent) - axis_at - 1))

    factor_of = one(*shards[0])
    for cut in shards[1:]:
        factor_of = factor_of * one(*cut)
    return factor_of


def normal_values(rng, shape, spread, bound, shards=(), kind=jnp.bfloat16):
    entries = spread * jax.random.normal(rng, shape, jnp.float32)
    if shards:
        entries = entries * levels(rng, shape, shards, -0.22, 0.18)
    return jnp.clip(entries, -bound, bound).astype(kind)


def setup_inputs(seed: int = 0) -> dict:
    streams_of = jax.random.split(jax.random.key(seed), 6)
    return {
        "init": normal_values(streams_of[0], (NZ, NX, NY), 1.0, 6.0, ((0, 8), (2, 4)), jnp.float32),
        "measured": draw_measured(jax.random.fold_in(streams_of[5], 71), 0),
        "mask": draw_mask(jax.random.fold_in(streams_of[5], 71), 0),
        "kernel_index": with_ends(jax.random.randint(streams_of[3], (VIEWS, ZBANDS, XBLOCKS), 0, NK), jax.random.fold_in(streams_of[3], 1), 0, NK - 1).astype(jnp.int32),
        "kernels": jnp.clip(jnp.exp(jax.random.uniform(streams_of[4], (NK, TAPS), jnp.float32, math.log(0.02), math.log(0.3))), 0.02, 0.3),
    }


HIGHEST = lax.Precision.HIGHEST
damping = 1.0


def blur_tables(kernel_index, kernels):
    onehot = (kernel_index[..., None] == jnp.arange(NK, dtype=jnp.int32)).astype(jnp.float32)
    tap_values = jnp.einsum("vabk,kt->vabt", onehot, kernels.astype(jnp.float32), precision=HIGHEST)
    row_taps = jnp.repeat(tap_values, ZBW, axis=1)
    depths = jnp.arange(NZ, dtype=jnp.int32)
    offset = depths[None, :] - depths[:, None] + HALF
    tap_select = (offset[:, :, None] == jnp.arange(TAPS, dtype=jnp.int32)).astype(jnp.float32)
    return jnp.einsum("vzbt,zwt->vbzw", row_taps, tap_select, precision=HIGHEST)


def reference(init, measured, mask, kernel_index, kernels):
    blur_mats = blur_tables(kernel_index, kernels)
    gram_mats = jnp.einsum("vbzw,vbzu->bwu", blur_mats, blur_mats, precision=HIGHEST)
    band_count = NX // BX
    projected = jnp.zeros((NZ, band_count, BX, NY), jnp.float32)
    for view_index in range(VIEWS):
        view_data = measured[view_index].reshape(NZ, band_count, BX, NY)
        projected = projected + jnp.einsum("bzw,zbxy->wbxy", blur_mats[view_index], view_data, precision=HIGHEST)
    projected = projected.reshape(NZ, NX, NY)
    tissue = jnp.repeat(jnp.repeat(mask.astype(jnp.float32), BX, axis=0), BY, axis=1)

    def apply_gram(field):
        product = jnp.einsum("bwz,zbxy->wbxy", gram_mats, field.reshape(NZ, band_count, BX, NY), precision=HIGHEST)
        return product.reshape(NZ, NX, NY)

    def operate(field):
        return damping * field + tissue * apply_gram(field)

    solved = init
    residual = tissue * (projected - apply_gram(init))
    direction = residual
    norm_now = jnp.sum(residual * residual)
    for iteration in range(ITERS):
        image_field = operate(direction)
        step_size = norm_now / jnp.sum(direction * image_field)
        solved = solved + step_size * direction
        residual = residual - step_size * image_field
        norm_next = jnp.sum(residual * residual)
        direction = residual + (norm_next / norm_now) * direction
        norm_now = norm_next
    return solved
```

```python
import functools

import jax
import jax.numpy as jnp
from jax import lax
from jax.experimental import pallas as pl
from jax.experimental.pallas import tpu as pltpu
from jax.sharding import PartitionSpec as P

ITERS = 4
MOMENTS = 2 * ITERS

HIGHEST = lax.Precision.HIGHEST
damping = 1.0
MIB = 1 << 20


def blur_tables(kernel_index, kernels, depth):
    bank, taps = kernels.shape
    width = depth // kernel_index.shape[1]
    onehot = (kernel_index[..., None] == jnp.arange(bank, dtype=jnp.int32)).astype(jnp.float32)
    tap_values = jnp.einsum("vabk,kt->vabt", onehot, kernels, precision=HIGHEST)
    row_taps = jnp.repeat(tap_values, width, axis=1)
    depths = jnp.arange(depth, dtype=jnp.int32)
    offset = depths[None, :] - depths[:, None] + taps // 2
    tap_select = (offset[:, :, None] == jnp.arange(taps, dtype=jnp.int32)).astype(jnp.float32)
    return jnp.einsum("vzbt,zwt->vbzw", row_taps, tap_select, precision=HIGHEST)


def split(x):
    high = x.astype(jnp.bfloat16)
    return high, (x - high.astype(jnp.float32)).astype(jnp.bfloat16)


def left_operand(matrix):
    high, low = split(matrix)
    return jnp.concatenate(
        [jnp.concatenate([high, high], axis=1), jnp.concatenate([low, low], axis=1)], axis=0
    )


def right_operand(matrix):
    return jnp.concatenate(split(matrix), axis=0)


def product(left, right):
    both = jnp.dot(left, right, preferred_element_type=jnp.float32)
    rows = both.shape[0] // 2
    return both[:rows] + both[rows:]


def tissue_half(mask_ref, tile):
    return mask_ref[tile, 2 * lax.axis_index("gy") + 1]


def tissue_lanes(shape, half):
    lane = lax.broadcasted_iota(jnp.int32, shape, len(shape) - 1)
    return (lane >= shape[-1] // 2) == (half == 1)


def pack_kernel(mask_ref, init_ref, *refs):
    count = len(refs) - 2
    out_refs, staged, sems = refs[:count], refs[count], refs[count + 1]
    slab, columns, lanes = out_refs[0].shape
    width = 2 * columns
    me = lax.axis_index("gz")

    def copy(k):
        tile = jnp.bitwise_xor(me, k)
        start = pl.multiple_of(tile * width, width)
        return pltpu.make_async_copy(
            init_ref.at[:, pl.ds(start, width), :], staged.at[k], sems.at[k]
        )

    for k in range(count):
        copy(k).start()
    for k in range(count):
        copy(k).wait()
        half = tissue_half(mask_ref, jnp.bitwise_xor(me, k))
        here = tissue_lanes((slab, columns, lanes), half)
        first = staged[k, :, :columns, :]
        second = pltpu.roll(staged[k, :, columns:, :], lanes // 2, 2)
        out_refs[k][...] = jnp.where(here, first, second)


def project_kernel(mask_ref, blur_ref, first_ref, second_ref, out_ref, left_ref):
    views, depth, columns, lanes = first_ref.shape

    @pl.when(pl.program_id(0) == 0)
    def _():
        for v in range(views):
            left_ref[:, 2 * depth * v : 2 * depth * (v + 1)] = left_operand(blur_ref[v].T)

    half = tissue_half(mask_ref, lax.axis_index("gz"))
    here = tissue_lanes((depth, lanes), half)
    rows = views * depth * columns
    first = first_ref.reshape(rows, lanes)
    second = second_ref.reshape(rows, lanes)

    def packed(v, x):
        at = pl.ds(v * depth * columns + x, depth, stride=columns)
        return jnp.where(here, first[at, :], pltpu.roll(second[at, :], lanes // 2, 1))

    for x in range(0, columns, 2):
        parts = []
        for v in range(views):
            parts.append(right_operand(jnp.concatenate([packed(v, x), packed(v, x + 1)], axis=1)))
        result = product(left_ref[...], jnp.concatenate(parts, axis=0))
        out_ref[x] = result[:, :lanes]
        out_ref[x + 1] = result[:, lanes:]


def residual_kernel(gram_ref, poly_ref, projected_ref, *refs):
    count = len(refs) - 4
    chunks, residual_ref, moments_ref, left_ref, square_ref = (
        refs[:count],
        refs[count],
        refs[count + 1],
        refs[count + 2],
        refs[count + 3],
    )
    slab, columns, lanes = chunks[0].shape
    left_ref[...] = left_operand(gram_ref[...])
    square_ref[...] = jnp.zeros_like(square_ref)
    flat = [chunk.reshape(slab * columns, lanes) for chunk in chunks]

    def field(x):
        return jnp.concatenate([ref[pl.ds(x, slab, stride=columns), :] for ref in flat], axis=0)

    @pl.loop(0, columns // 2)
    def _(pair):
        x = 2 * pair
        image = product(
            left_ref[...], right_operand(jnp.concatenate([field(x), field(x + 1)], axis=1))
        )
        start = jnp.concatenate([projected_ref[x], projected_ref[x + 1]], axis=1)
        both = right_operand(start - image)
        residual_ref[pair] = both
        square_ref[...] += lax.dot_general(
            both, both, (((1,), (1,)), ((), ())), preferred_element_type=jnp.float32
        )

    depth = gram_ref.shape[0]
    square = square_ref[...]
    square = (square[:depth, :depth] + square[depth:, depth:]) + (
        square[:depth, depth:] + square[depth:, :depth]
    )
    lane = lax.broadcasted_iota(jnp.int32, (1, lanes), 1)
    row = jnp.zeros((1, lanes), jnp.float32)
    for k in range(poly_ref.shape[0]):
        total = jnp.sum(jnp.sum(square * poly_ref[k], axis=0, keepdims=True), axis=1, keepdims=True)
        row = jnp.where(lane == k, total, row)
    moments_ref[...] = jnp.broadcast_to(row, moments_ref.shape)


def conjugate(moments, centre, radius):
    def inner(p, q):
        total = None
        for i, a in enumerate(p):
            for j, b in enumerate(q):
                term = a * b * (0.5 * (moments[i + j] + moments[abs(i - j)]))
                total = term if total is None else total + term
        return total

    def operate(p):
        image = [centre * a for a in p] + [None]

        def put(i, value):
            image[i] = value if image[i] is None else image[i] + value

        for j, a in enumerate(p):
            if j == 0:
                put(1, radius * a)
            else:
                put(j + 1, 0.5 * radius * a)
                put(j - 1, 0.5 * radius * a)
        return image

    one = jnp.ones_like(moments[0])
    residual, direction = [one], [one]
    solved = []
    norm_now = moments[0]
    for iteration in range(ITERS):
        image = operate(direction)
        step_size = norm_now / inner(direction, image)
        solved = [s + step_size * d for s, d in zip(solved, direction)] + [
            step_size * d for d in direction[len(solved) :]
        ]
        if iteration == ITERS - 1:
            break
        residual = [r - step_size * i for r, i in zip(residual, image)] + [
            -step_size * i for i in image[len(residual) :]
        ]
        norm_next = inner(residual, residual)
        ratio = norm_next / norm_now
        direction = [r + ratio * d for r, d in zip(residual, direction)] + residual[len(direction) :]
        norm_now = norm_next
    return solved


def correct_kernel(top_ref, moments_ref, poly_ref, residual_ref, *refs):
    count = len(refs) - 1
    out_refs, left_ref = refs[:count], refs[count]
    slab, columns, lanes = out_refs[0].shape
    row = jnp.sum(moments_ref[...], axis=0, keepdims=True)
    lane = lax.broadcasted_iota(jnp.int32, row.shape, 1)
    moments = [
        jnp.sum(jnp.where(lane == k, row, 0.0), axis=1, keepdims=True) for k in range(MOMENTS)
    ]
    radius = 0.5 * top_ref[...]
    coefficients = conjugate(moments, damping + radius, radius)
    matrix = coefficients[0] * poly_ref[0]
    for k in range(1, ITERS):
        matrix = matrix + coefficients[k] * poly_ref[k]
    left_ref[...] = left_operand(matrix)
    flat = [ref.reshape(slab * columns, lanes) for ref in out_refs]

    @pl.loop(0, columns // 2)
    def _(pair):
        result = product(left_ref[...], residual_ref[pair])
        for k in range(count):
            rows = result[slab * k : slab * (k + 1)]
            for side in range(2):
                flat[k][pl.ds(2 * pair + side, slab, stride=columns), :] = rows[
                    :, lanes * side : lanes * (side + 1)
                ]


def unpack_kernel(group, aliased, mask_ref, init_ref, *refs):
    if aliased:
        refs = refs[1:]
    chunks, (out_ref, staged, in_sems, out_sems) = refs[:-4], refs[-4:]
    slab, columns, lanes = chunks[0].shape
    width = 2 * columns
    me = lax.axis_index("gz")

    def tile(k):
        return jnp.bitwise_xor(me, k)

    def columns_of(ref, k):
        return ref.at[:, pl.ds(pl.multiple_of(tile(k) * width, width), width), :]

    loads = [
        pltpu.make_async_copy(columns_of(init_ref, k), staged.at[n], in_sems.at[n])
        for n, k in enumerate(group)
    ]
    stores = [
        pltpu.make_async_copy(staged.at[n], columns_of(out_ref, k), out_sems.at[n])
        for n, k in enumerate(group)
    ]
    for load in loads:
        load.start()
    for n, k in enumerate(group):
        here = tissue_lanes((slab, columns, lanes), tissue_half(mask_ref, tile(k)))
        change = chunks[n][...]
        loads[n].wait()
        staged[n, :, :columns, :] += jnp.where(here, change, 0.0)
        staged[n, :, columns:, :] += pltpu.roll(jnp.where(here, 0.0, change), lanes // 2, 2)
        stores[n].start()
    for store in stores:
        store.wait()


SMEM = pl.BlockSpec(memory_space=pltpu.SMEM)
VMEM = pl.BlockSpec(memory_space=pltpu.VMEM)
ANY = pl.BlockSpec(memory_space=pl.ANY)


def local(init, measured, mask, kernel_index, kernels):
    tiles, rows = lax.axis_size("gz"), lax.axis_size("gy")
    slab, _, lanes = init.shape
    views, depth, width, _ = measured.shape
    columns = width // 2
    me = lax.axis_index("gz")
    f32 = jnp.float32
    chunk = jax.ShapeDtypeStruct((slab, columns, lanes), f32)

    def exchange(chunks):
        return [chunks[0]] + [
            lax.ppermute(chunks[k], "gz", [(j, j ^ k) for j in range(tiles)])
            for k in range(1, tiles)
        ]

    packed = pl.pallas_call(
        pack_kernel,
        name="pack_blocks",
        out_shape=[chunk] * tiles,
        in_specs=[SMEM, ANY],
        out_specs=[VMEM] * tiles,
        scratch_shapes=[
            pltpu.VMEM((tiles, slab, width, lanes), f32),
            pltpu.SemaphoreType.DMA((tiles,)),
        ],
        compiler_params=pltpu.CompilerParams(vmem_limit_bytes=32 * MIB),
        cost_estimate=pl.CostEstimate(
            flops=init.size, bytes_accessed=6 * init.size, transcendentals=0
        ),
    )(mask, init)
    fields = exchange(packed)

    blurs = blur_tables(kernel_index, kernels, depth)
    row_sums = jnp.sum(blurs, axis=3)
    top = jnp.max(jnp.sum(blurs * row_sums[..., None], axis=(0, 2)))
    blur = lax.dynamic_index_in_dim(blurs, me, 1, False)
    gram = jnp.einsum("vzw,vzu->wu", blur, blur, precision=HIGHEST)

    step = 8
    projected = pl.pallas_call(
        project_kernel,
        name="project_views",
        grid=(columns // step,),
        out_shape=jax.ShapeDtypeStruct((columns, depth, lanes), f32),
        in_specs=[
            SMEM,
            pl.BlockSpec((views, depth, depth), lambda i: (0, 0, 0)),
            pl.BlockSpec((views, depth, step, lanes), lambda i: (0, 0, i, 0)),
            pl.BlockSpec((views, depth, step, lanes), lambda i: (0, 0, i + columns // step, 0)),
        ],
        out_specs=pl.BlockSpec((step, depth, lanes), lambda i: (i, 0, 0)),
        scratch_shapes=[pltpu.VMEM((2 * depth, 2 * views * depth), jnp.bfloat16)],
        compiler_params=pltpu.CompilerParams(vmem_limit_bytes=32 * MIB),
        cost_estimate=pl.CostEstimate(
            flops=8 * views * depth * depth * columns * lanes,
            bytes_accessed=4 * measured.size,
            transcendentals=0,
        ),
    )(mask, blur, measured, measured)

    eye = jnp.eye(depth, dtype=f32)
    poly = [eye, gram * (2.0 / top) - eye]
    for k in range(2, MOMENTS):
        half = k // 2
        other = k - half
        poly.append(
            2.0 * jnp.dot(poly[other], poly[half], precision=HIGHEST) - poly[other - half]
        )
    depths = jnp.arange(depth, dtype=jnp.int32)
    source = jnp.bitwise_xor(me, depths // slab) * slab + depths % slab
    order = (source[:, None] == depths[None, :]).astype(f32)
    gram_in = jnp.dot(gram, order.T, precision=HIGHEST)
    poly_out = jnp.stack(
        [jnp.dot(order, poly[k], precision=HIGHEST) for k in range(ITERS)]
    )
    poly = jnp.stack(poly)

    everyone = tiles * rows
    pairs = columns // 2
    residual, moments = pl.pallas_call(
        residual_kernel,
        name="first_residual",
        out_shape=[
            jax.ShapeDtypeStruct((pairs, 2 * depth, 2 * lanes), jnp.bfloat16),
            jax.ShapeDtypeStruct((everyone, lanes), f32),
        ],
        in_specs=[VMEM] * (3 + tiles),
        out_specs=[VMEM] * 2,
        scratch_shapes=[
            pltpu.VMEM((2 * depth, 2 * depth), jnp.bfloat16),
            pltpu.VMEM((2 * depth, 2 * depth), f32),
        ],
        compiler_params=pltpu.CompilerParams(vmem_limit_bytes=32 * MIB),
        cost_estimate=pl.CostEstimate(
            flops=16 * depth * depth * columns * lanes,
            bytes_accessed=12 * depth * columns * lanes,
            transcendentals=0,
        ),
    )(gram_in, poly, projected, *fields)

    moments = lax.all_to_all(moments, ("gz", "gy"), split_axis=0, concat_axis=0, tiled=True)

    changes = pl.pallas_call(
        correct_kernel,
        name="correction",
        out_shape=[chunk] * tiles,
        in_specs=[VMEM] * 4,
        out_specs=[VMEM] * tiles,
        scratch_shapes=[pltpu.VMEM((2 * depth, 2 * depth), jnp.bfloat16)],
        compiler_params=pltpu.CompilerParams(vmem_limit_bytes=32 * MIB),
        cost_estimate=pl.CostEstimate(
            flops=8 * depth * depth * columns * lanes,
            bytes_accessed=8 * depth * columns * lanes,
            transcendentals=0,
        ),
    )(top.reshape(1, 1), moments, poly_out, residual)
    changes = exchange(changes)

    solved = None
    group_size = max(1, tiles // 4)
    for first in range(0, tiles, group_size):
        group = list(range(first, first + group_size))
        solved = pl.pallas_call(
            functools.partial(unpack_kernel, group, solved is not None),
            name="add_correction",
            out_shape=jax.ShapeDtypeStruct(init.shape, f32),
            in_specs=[SMEM, ANY] + [ANY] * (solved is not None) + [VMEM] * group_size,
            out_specs=ANY,
            input_output_aliases={} if solved is None else {2: 0},
            scratch_shapes=[
                pltpu.VMEM((group_size, slab, width, lanes), f32),
                pltpu.SemaphoreType.DMA((group_size,)),
                pltpu.SemaphoreType.DMA((group_size,)),
            ],
            compiler_params=pltpu.CompilerParams(vmem_limit_bytes=32 * MIB),
            cost_estimate=pl.CostEstimate(
                flops=init.size, bytes_accessed=10 * init.size // 4, transcendentals=0
            ),
        )(mask, init, *([] if solved is None else [solved]), *[changes[k] for k in group])
    return solved


def solution(mesh):
    return jax.shard_map(
        local,
        mesh=mesh,
        in_specs=(P("gz", None, "gy"), P(None, None, "gz", "gy"), P(), P(), P()),
        out_specs=P("gz", None, "gy"),
        check_vma=False,
    )
```

```python
import functools

import jax
import jax.numpy as jnp
from jax import lax
from jax.experimental import pallas as pl
from jax.experimental.pallas import tpu as pltpu
from jax.sharding import PartitionSpec as P

ITERS = 4
MOMENTS = 2 * ITERS

HIGHEST = lax.Precision.HIGHEST
damping = 1.0
MIB = 1 << 20
UNROLL = 4
IN_FLIGHT = 5


def split(x):
    high = x.astype(jnp.bfloat16)
    return high, (x - high.astype(jnp.float32)).astype(jnp.bfloat16)


def left_operand(matrix):
    high, low = split(matrix)
    return jnp.concatenate(
        [jnp.concatenate([high, high], axis=1), jnp.concatenate([low, low], axis=1)], axis=0
    )


def right_operand(matrix):
    return jnp.concatenate(split(matrix), axis=0)


def product(left, right):
    both = jnp.dot(left, right, preferred_element_type=jnp.float32)
    rows = both.shape[0] // 2
    return both[:rows] + both[rows:]


def tissue_half(mask_ref, tile):
    return mask_ref[tile, 2 * lax.axis_index("gy") + 1]


def tissue_lanes(shape, half):
    lane = lax.broadcasted_iota(jnp.int32, shape, len(shape) - 1)
    return (lane >= shape[-1] // 2) == (half == 1)


def pack_kernel(mask_ref, init_ref, *refs):
    count = len(refs) - 4
    out_refs, (staged, flags, sems, flag_sem) = refs[:count], refs[count:]
    slab, columns, lanes = out_refs[0].shape
    width = 2 * columns
    me = lax.axis_index("gz")

    def copy(k):
        start = pl.multiple_of(jnp.bitwise_xor(me, k) * width, width)
        return pltpu.make_async_copy(
            init_ref.at[:, pl.ds(start, width), :], staged.at[k], sems.at[k]
        )

    flag_copy = pltpu.make_async_copy(mask_ref, flags, flag_sem)
    flag_copy.start()
    for k in range(count):
        copy(k).start()
    flag_copy.wait()
    for k in range(count):
        copy(k).wait()
        half = tissue_half(flags, jnp.bitwise_xor(me, k))
        here = tissue_lanes((slab, columns, lanes), half)
        first = staged[k, :, :columns, :]
        second = pltpu.roll(staged[k, :, columns:, :], lanes // 2, 2)
        out_refs[k][...] = jnp.where(here, first, second)


def tables_kernel(
    index_ref, kernels_ref, left_ref, gram_ref, poly_ref, top_ref, bank, boxes, blur, square
):
    views, zbands, xbands = index_ref.shape
    taps = kernels_ref.shape[1]
    depth = poly_ref.shape[-1]
    zwidth = depth // zbands
    reach = taps // 2
    me = lax.axis_index("gz")

    def pick(ref, v, zband, xband):
        return ref[pl.ds(index_ref[v, zband, xband], 1), :]

    bank[...] = jnp.zeros_like(bank)
    bank[:, :taps] = kernels_ref[...]
    rows = bank[...]
    box = rows
    for r in range(1, zwidth):
        box = box + pltpu.roll(rows, r, 1)
    boxes[...] = box * jnp.sum(rows, axis=1, keepdims=True)

    def row_sums(xband, largest):
        total = jnp.zeros((1, depth), jnp.float32)
        for zband in range(zbands):
            part = pick(boxes, 0, zband, xband)
            for v in range(1, views):
                part = part + pick(boxes, v, zband, xband)
            total = total + pltpu.roll(part, (zband * zwidth - reach) % depth, 1)
        return jnp.maximum(largest, total)

    largest = lax.fori_loop(0, xbands, row_sums, jnp.zeros((1, depth), jnp.float32))
    top = jnp.max(largest, axis=1, keepdims=True)
    top_ref[...] = jnp.broadcast_to(top, top_ref.shape)

    z = lax.broadcasted_iota(jnp.int32, (zwidth, depth), 0)
    w = lax.broadcasted_iota(jnp.int32, (zwidth, depth), 1)
    for v in range(views):
        for zband in range(zbands):
            first = zband * zwidth
            row = jnp.broadcast_to(pick(bank, v, zband, me), (zwidth, depth))
            row = pltpu.roll(row, (first - reach) % depth, 1, stride=1, stride_axis=0)
            blur[v * depth + first : v * depth + first + zwidth, :] = jnp.where(
                jnp.abs(w - z - first) <= reach, row, 0.0
            )
    across = blur[...].T
    for v in range(views):
        left_ref[:, 2 * depth * v : 2 * depth * (v + 1)] = left_operand(
            across[:, depth * v : depth * (v + 1)]
        )
    gram = jnp.dot(across, blur[...], precision=HIGHEST, preferred_element_type=jnp.float32)
    square[...] = gram
    tiles = xbands
    slab = depth // tiles
    swapped = jnp.concatenate(
        [square[pl.ds(pl.multiple_of(jnp.bitwise_xor(me, k) * slab, slab), slab), :] for k in range(tiles)],
        axis=0,
    )
    gram_ref[...] = left_operand(swapped.T)

    eye = jnp.where(
        lax.broadcasted_iota(jnp.int32, (depth, depth), 0)
        == lax.broadcasted_iota(jnp.int32, (depth, depth), 1),
        1.0,
        0.0,
    )
    poly = [eye, gram * (2.0 / top) - eye]
    for k in range(2, MOMENTS):
        half = k // 2
        other = k - half
        poly.append(
            2.0
            * jnp.dot(
                poly[other], poly[half], precision=HIGHEST, preferred_element_type=jnp.float32
            )
            - poly[other - half]
        )
    for k in range(MOMENTS):
        poly_ref[k] = poly[k]


def project_kernel(mask_ref, left_ref, measured_ref, out_ref, staged, sems):
    _, _, views, depth, step, lanes = staged.shape
    columns = out_ref.shape[0]
    steps = columns // step

    def copy(i, side):
        start = pl.multiple_of(i * step + side * columns, step)
        return pltpu.make_async_copy(
            measured_ref.at[:, :, pl.ds(start, step), :],
            staged.at[i % 2, side],
            sems.at[i % 2, side],
        )

    for side in range(2):
        copy(0, side).start()
    half = tissue_half(mask_ref, lax.axis_index("gz"))
    here = tissue_lanes((depth, lanes), half)
    flat = staged.reshape(2 * 2 * views * depth * step, lanes)

    @pl.loop(0, steps)
    def _(i):
        @pl.when(i + 1 < steps)
        def _():
            for side in range(2):
                copy(i + 1, side).start()

        for side in range(2):
            copy(i, side).wait()

        def read(side, v, x):
            start = (((i % 2) * 2 + side) * views + v) * (depth * step) + x
            return flat[pl.ds(start, depth, stride=step), :]

        def packed(v, x):
            return jnp.where(here, read(0, v, x), pltpu.roll(read(1, v, x), lanes // 2, 1))

        for x in range(0, step, 2):
            parts = []
            for v in range(views):
                parts.append(
                    right_operand(jnp.concatenate([packed(v, x), packed(v, x + 1)], axis=1))
                )
            result = product(left_ref[...], jnp.concatenate(parts, axis=0))
            out_ref[i * step + x] = result[:, :lanes]
            out_ref[i * step + x + 1] = result[:, lanes:]


def residual_kernel(gram_ref, poly_ref, projected_ref, *refs):
    count = len(refs) - 3
    chunks, (residual_ref, moments_ref, square_ref) = refs[:count], refs[count:]
    slab, columns, lanes = chunks[0].shape
    depth = poly_ref.shape[-1]
    square_ref[...] = jnp.zeros_like(square_ref)
    flat = [chunk.reshape(slab * columns, lanes) for chunk in chunks]

    def field(x):
        return jnp.concatenate([ref[pl.ds(x, slab, stride=columns), :] for ref in flat], axis=0)

    @pl.loop(0, columns // 2, step=UNROLL)
    def _(first):
        total = None
        for i in range(UNROLL):
            pair = first + i
            x = 2 * pair
            image = product(
                gram_ref[...], right_operand(jnp.concatenate([field(x), field(x + 1)], axis=1))
            )
            start = jnp.concatenate([projected_ref[x], projected_ref[x + 1]], axis=1)
            both = right_operand(start - image)
            residual_ref[pair] = both
            square = lax.dot_general(
                both, both, (((1,), (1,)), ((), ())), preferred_element_type=jnp.float32
            )
            total = square if total is None else total + square
        square_ref[...] += total

    square = square_ref[...]
    square = (square[:depth, :depth] + square[depth:, depth:]) + (
        square[:depth, depth:] + square[depth:, :depth]
    )
    count = poly_ref.shape[0]
    sums = jnp.concatenate(
        [jnp.sum(square * poly_ref[k], axis=0, keepdims=True) for k in range(count)], axis=0
    )
    sums = jnp.sum(sums, axis=1, keepdims=True)
    lane = lax.broadcasted_iota(jnp.int32, (count, lanes), 1)
    order = lax.broadcasted_iota(jnp.int32, (count, lanes), 0)
    row = jnp.sum(jnp.where(lane == order, sums, 0.0), axis=0, keepdims=True)
    moments_ref[...] = jnp.broadcast_to(row, moments_ref.shape)


def conjugate(moments, centre, radius):
    def inner(p, q):
        total = None
        for i, a in enumerate(p):
            for j, b in enumerate(q):
                term = a * b * (0.5 * (moments[i + j] + moments[abs(i - j)]))
                total = term if total is None else total + term
        return total

    def operate(p):
        image = [centre * a for a in p] + [None]

        def put(i, value):
            image[i] = value if image[i] is None else image[i] + value

        for j, a in enumerate(p):
            if j == 0:
                put(1, radius * a)
            else:
                put(j + 1, 0.5 * radius * a)
                put(j - 1, 0.5 * radius * a)
        return image

    one = jnp.ones_like(moments[0])
    residual, direction = [one], [one]
    solved = []
    norm_now = moments[0]
    for iteration in range(ITERS):
        image = operate(direction)
        step_size = norm_now / inner(direction, image)
        solved = [s + step_size * d for s, d in zip(solved, direction)] + [
            step_size * d for d in direction[len(solved) :]
        ]
        if iteration == ITERS - 1:
            break
        residual = [r - step_size * i for r, i in zip(residual, image)] + [
            -step_size * i for i in image[len(residual) :]
        ]
        norm_next = inner(residual, residual)
        ratio = norm_next / norm_now
        direction = [r + ratio * d for r, d in zip(residual, direction)] + residual[len(direction) :]
        norm_now = norm_next
    return solved


def correct_kernel(top_ref, moments_ref, poly_ref, residual_ref, *refs):
    count = len(refs) - 2
    out_refs, (matrix_ref, left_ref) = refs[:count], refs[count:]
    slab, columns, lanes = out_refs[0].shape
    me = lax.axis_index("gz")
    row = jnp.sum(moments_ref[...], axis=0, keepdims=True)
    lane = lax.broadcasted_iota(jnp.int32, row.shape, 1)
    moments = [
        jnp.sum(jnp.where(lane == k, row, 0.0), axis=1, keepdims=True) for k in range(MOMENTS)
    ]
    radius = 0.5 * top_ref[:1, :1]
    coefficients = conjugate(moments, damping + radius, radius)
    matrix = coefficients[0] * poly_ref[0]
    for k in range(1, ITERS):
        matrix = matrix + coefficients[k] * poly_ref[k]
    matrix_ref[...] = matrix
    left_ref[...] = left_operand(
        jnp.concatenate(
            [
                matrix_ref[pl.ds(pl.multiple_of(jnp.bitwise_xor(me, k) * slab, slab), slab), :]
                for k in range(count)
            ],
            axis=0,
        )
    )
    flat = [ref.reshape(slab * columns, lanes) for ref in out_refs]

    @pl.loop(0, columns // 2, step=UNROLL)
    def _(first):
        for i in range(UNROLL):
            pair = first + i
            result = product(left_ref[...], residual_ref[pair])
            for k in range(count):
                rows = result[slab * k : slab * (k + 1)]
                for side in range(2):
                    flat[k][pl.ds(2 * pair + side, slab, stride=columns), :] = rows[
                        :, lanes * side : lanes * (side + 1)
                    ]


def unpack_kernel(group, aliased, mask_ref, init_ref, *refs):
    if aliased:
        refs = refs[1:]
    chunks, (out_ref, staged, in_sems, out_sems) = refs[:-4], refs[-4:]
    slab, columns, lanes = chunks[0].shape
    width = 2 * columns
    me = lax.axis_index("gz")

    def tile(k):
        return jnp.bitwise_xor(me, k)

    def columns_of(ref, k):
        return ref.at[:, pl.ds(pl.multiple_of(tile(k) * width, width), width), :]

    loads = [
        pltpu.make_async_copy(columns_of(init_ref, k), staged.at[n], in_sems.at[n])
        for n, k in enumerate(group)
    ]
    stores = [
        pltpu.make_async_copy(staged.at[n], columns_of(out_ref, k), out_sems.at[n])
        for n, k in enumerate(group)
    ]
    for load in loads:
        load.start()
    for n, k in enumerate(group):
        here = tissue_lanes((slab, columns, lanes), tissue_half(mask_ref, tile(k)))
        change = chunks[n][...]
        loads[n].wait()
        staged[n, :, :columns, :] += jnp.where(here, change, 0.0)
        staged[n, :, columns:, :] += pltpu.roll(jnp.where(here, 0.0, change), lanes // 2, 2)
        stores[n].start()
    for store in stores:
        store.wait()


SMEM = pl.BlockSpec(memory_space=pltpu.SMEM)
VMEM = pl.BlockSpec(memory_space=pltpu.VMEM)
HBM = pl.BlockSpec(memory_space=pltpu.HBM)
ANY = pl.BlockSpec(memory_space=pl.ANY)


def cost(flops, read, transcendentals=0):
    return pl.CostEstimate(
        flops=int(flops), bytes_accessed=int(read), transcendentals=transcendentals
    )


def local(init, measured, mask, kernel_index, kernels):
    tiles, rows = lax.axis_size("gz"), lax.axis_size("gy")
    slab, _, lanes = init.shape
    views, depth, width, _ = measured.shape
    columns = width // 2
    f32, bf16 = jnp.float32, jnp.bfloat16
    shape = jax.ShapeDtypeStruct
    chunk = shape((slab, columns, lanes), f32)

    def send(block, k):
        return lax.ppermute(block, "gz", [(j, j ^ k) for j in range(tiles)])

    packed = pl.pallas_call(
        pack_kernel,
        name="pack_blocks",
        out_shape=[chunk] * tiles,
        in_specs=[HBM, HBM],
        out_specs=[VMEM] * tiles,
        scratch_shapes=[
            pltpu.VMEM((tiles, slab, width, lanes), f32),
            pltpu.SMEM(mask.shape, jnp.int32),
            pltpu.SemaphoreType.DMA((tiles,)),
            pltpu.SemaphoreType.DMA,
        ],
        compiler_params=pltpu.CompilerParams(vmem_limit_bytes=60 * MIB),
        cost_estimate=cost(init.size, 6 * init.size),
    )(mask, init)

    order = [1] + [k for k in range(tiles - 2, 1, -1) if k % 2 == 0]
    order += [k for k in range(tiles - 1, 1, -1) if k % 2 == 1]
    fields = [packed[0]] + [None] * (tiles - 1)
    for n, k in enumerate(order):
        block = packed[k]
        if n >= IN_FLIGHT:
            before = order[n - IN_FLIGHT]
            block, fields[before] = lax.optimization_barrier((block, fields[before]))
        fields[k] = send(block, k)

    poly_shape = shape((MOMENTS, depth, depth), f32)
    left, gram, poly, top = pl.pallas_call(
        tables_kernel,
        name="blur_tables",
        out_shape=[
            shape((2 * depth, 2 * views * depth), bf16),
            shape((2 * depth, 2 * depth), bf16),
            poly_shape,
            shape((8, lanes), f32),
        ],
        in_specs=[SMEM, VMEM],
        out_specs=[VMEM] * 4,
        scratch_shapes=[
            pltpu.VMEM((kernels.shape[0], depth), f32),
            pltpu.VMEM((kernels.shape[0], depth), f32),
            pltpu.VMEM((views * depth, depth), f32),
            pltpu.VMEM((depth, depth), f32),
        ],
        compiler_params=pltpu.CompilerParams(vmem_limit_bytes=8 * MIB),
        cost_estimate=cost(12 * 20 * depth**3, 4 * MIB),
    )(kernel_index, kernels)

    step = 8
    projected = pl.pallas_call(
        project_kernel,
        name="project_views",
        out_shape=shape((columns, depth, lanes), f32),
        in_specs=[SMEM, VMEM, HBM],
        out_specs=VMEM,
        scratch_shapes=[
            pltpu.VMEM((2, 2, views, depth, step, lanes), f32),
            pltpu.SemaphoreType.DMA((2, 2)),
        ],
        compiler_params=pltpu.CompilerParams(vmem_limit_bytes=48 * MIB),
        cost_estimate=cost(8 * views * depth * depth * columns * lanes, 4 * measured.size),
    )(mask, left, measured)

    everyone = tiles * rows
    pairs = columns // 2
    residual, moments = pl.pallas_call(
        residual_kernel,
        name="first_residual",
        out_shape=[
            shape((pairs, 2 * depth, 2 * lanes), bf16),
            shape((everyone, lanes), f32),
        ],
        in_specs=[VMEM] * (3 + tiles),
        out_specs=[VMEM] * 2,
        scratch_shapes=[pltpu.VMEM((2 * depth, 2 * depth), f32)],
        compiler_params=pltpu.CompilerParams(vmem_limit_bytes=16 * MIB),
        cost_estimate=cost(
            16 * depth * depth * columns * lanes, 12 * depth * columns * lanes
        ),
    )(gram, poly, projected, *fields)

    moments = lax.all_to_all(moments, ("gz", "gy"), split_axis=0, concat_axis=0, tiled=True)

    changes = pl.pallas_call(
        correct_kernel,
        name="correction",
        out_shape=[chunk] * tiles,
        in_specs=[VMEM] * 4,
        out_specs=[VMEM] * tiles,
        scratch_shapes=[
            pltpu.VMEM((depth, depth), f32),
            pltpu.VMEM((2 * depth, 2 * depth), bf16),
        ],
        compiler_params=pltpu.CompilerParams(vmem_limit_bytes=16 * MIB),
        cost_estimate=cost(8 * depth * depth * columns * lanes, 8 * depth * columns * lanes),
    )(top, moments, poly, residual)
    changes = [changes[0]] + [send(changes[k], k) for k in range(1, tiles)]

    cut = [0, tiles // 2, tiles // 2 + 1, tiles]
    groups = [list(range(first, last)) for first, last in zip(cut, cut[1:])]
    solved = None
    for group in groups:
        size = len(group)
        solved = pl.pallas_call(
            functools.partial(unpack_kernel, group, solved is not None),
            name="add_correction",
            out_shape=shape(init.shape, f32),
            in_specs=[SMEM, ANY] + [ANY] * (solved is not None) + [VMEM] * size,
            out_specs=ANY,
            input_output_aliases={} if solved is None else {2: 0},
            scratch_shapes=[
                pltpu.VMEM((size, slab, width, lanes), f32),
                pltpu.SemaphoreType.DMA((size,)),
                pltpu.SemaphoreType.DMA((size,)),
            ],
            compiler_params=pltpu.CompilerParams(vmem_limit_bytes=16 * MIB),
            cost_estimate=cost(init.size // 4, 5 * init.size // 4 * size),
        )(mask, init, *([] if solved is None else [solved]), *[changes[k] for k in group])
    return solved


def solution(mesh):
    return jax.shard_map(
        local,
        mesh=mesh,
        in_specs=(P("gz", None, "gy"), P(None, None, "gz", "gy"), P(), P(), P()),
        out_specs=P("gz", None, "gy"),
        check_vma=False,
    )
```

```python
import functools

import jax
import jax.numpy as jnp
from jax import lax
from jax.experimental import pallas as pl
from jax.experimental.pallas import tpu as pltpu
from jax.sharding import PartitionSpec as P

ITERS = 4
MOMENTS = 2 * ITERS

HIGHEST = lax.Precision.HIGHEST
damping = 1.0
MIB = 1 << 20
IN_FLIGHT = 5


def split(x):
    high = x.astype(jnp.bfloat16)
    return high, (x - high.astype(jnp.float32)).astype(jnp.bfloat16)


def left_operand(matrix):
    high, low = split(matrix)
    return jnp.concatenate(
        [jnp.concatenate([high, high], axis=1), jnp.concatenate([low, low], axis=1)], axis=0
    )


def right_operand(matrix):
    return jnp.concatenate(split(matrix), axis=0)


def product(left, right):
    both = jnp.dot(left, right, preferred_element_type=jnp.float32)
    rows = both.shape[0] // 2
    return both[:rows] + both[rows:]


def slots(tiles):
    high = (tiles.bit_length() - 2) // 2

    def swapped(k):
        across = k >> 1
        if 4 ** high * 2 != tiles:
            return k
        return ((((across & (2**high - 1)) << high) | (across >> high)) << 1) | (k & 1)

    same, other = list(range(2, tiles, 2)), list(range(3, tiles, 2))
    order = [0, 1] + same + other
    return [(k, swapped(k)) for k in order]


def receiver(me, slot):
    even, odd = slot
    return jnp.bitwise_xor(me, even if even == odd else jnp.where(me % 2 == 0, even, odd))


def sender(me, slot):
    even, odd = slot
    return receiver(me, slot if even % 2 == 0 else (odd, even))


def tissue_half(mask_ref, tile):
    return mask_ref[tile, 2 * lax.axis_index("gy") + 1]


def tissue_lanes(shape, half):
    lane = lax.broadcasted_iota(jnp.int32, shape, len(shape) - 1)
    return (lane >= shape[-1] // 2) == (half == 1)


def pack_kernel(targets, mask_ref, init_ref, *refs):
    count = len(targets)
    out_refs, (staged, flags, sems, flag_sem) = refs[:count], refs[count:]
    _, slab, width, lanes = staged.shape
    columns = width // 2
    me = lax.axis_index("gz")

    def copy(n):
        start = pl.multiple_of(receiver(me, targets[n]) * width, width)
        return pltpu.make_async_copy(
            init_ref.at[:, pl.ds(start, width), :], staged.at[n], sems.at[n]
        )

    flag_copy = pltpu.make_async_copy(mask_ref, flags, flag_sem)
    flag_copy.start()
    for n in range(count):
        copy(n).start()
    flag_copy.wait()
    for n in range(count):
        copy(n).wait()
        half = tissue_half(flags, receiver(me, targets[n]))
        here = tissue_lanes((columns, lanes), half)
        for z in range(slab):
            first = staged[n, z, :columns, :]
            second = pltpu.roll(staged[n, z, columns:, :], lanes // 2, 1)
            out_refs[n][pl.ds(z, columns, stride=slab), :] = jnp.where(here, first, second)


def tables_kernel(
    index_ref, kernels_ref, left_ref, gram_ref, poly_ref, top_ref, bank, boxes, blur, square
):
    views, zbands, xbands = index_ref.shape
    taps = kernels_ref.shape[1]
    depth = poly_ref.shape[-1]
    zwidth = depth // zbands
    reach = taps // 2
    me = lax.axis_index("gz")

    def pick(ref, v, zband, xband):
        return ref[pl.ds(index_ref[v, zband, xband], 1), :]

    bank[...] = jnp.zeros_like(bank)
    bank[:, :taps] = kernels_ref[...]
    rows = bank[...]
    box = rows
    for r in range(1, zwidth):
        box = box + pltpu.roll(rows, r, 1)
    boxes[...] = box * jnp.sum(rows, axis=1, keepdims=True)

    def row_sums(xband, largest):
        total = jnp.zeros((1, depth), jnp.float32)
        for zband in range(zbands):
            part = pick(boxes, 0, zband, xband)
            for v in range(1, views):
                part = part + pick(boxes, v, zband, xband)
            total = total + pltpu.roll(part, (zband * zwidth - reach) % depth, 1)
        return jnp.maximum(largest, total)

    largest = lax.fori_loop(0, xbands, row_sums, jnp.zeros((1, depth), jnp.float32))
    top = jnp.max(largest, axis=1, keepdims=True)
    top_ref[...] = jnp.broadcast_to(top, top_ref.shape)

    z = lax.broadcasted_iota(jnp.int32, (zwidth, depth), 0)
    w = lax.broadcasted_iota(jnp.int32, (zwidth, depth), 1)
    for v in range(views):
        for zband in range(zbands):
            first = zband * zwidth
            row = jnp.broadcast_to(pick(bank, v, zband, me), (zwidth, depth))
            row = pltpu.roll(row, (first - reach) % depth, 1, stride=1, stride_axis=0)
            blur[v * depth + first : v * depth + first + zwidth, :] = jnp.where(
                jnp.abs(w - z - first) <= reach, row, 0.0
            )
    across = blur[...].T
    for v in range(views):
        left_ref[:, 2 * depth * v : 2 * depth * (v + 1)] = left_operand(
            across[:, depth * v : depth * (v + 1)]
        )
    gram = jnp.dot(across, blur[...], precision=HIGHEST, preferred_element_type=jnp.float32)
    square[...] = gram
    tiles = xbands
    slab = depth // tiles
    swapped = jnp.concatenate(
        [
            square[pl.ds(pl.multiple_of(sender(me, slot) * slab, slab), slab), :]
            for slot in slots(tiles)
        ],
        axis=0,
    )
    gram_ref[...] = left_operand(swapped.T)

    eye = jnp.where(
        lax.broadcasted_iota(jnp.int32, (depth, depth), 0)
        == lax.broadcasted_iota(jnp.int32, (depth, depth), 1),
        1.0,
        0.0,
    )
    poly = [eye, gram * (2.0 / top) - eye]
    for k in range(2, MOMENTS):
        half = k // 2
        other = k - half
        poly.append(
            2.0
            * jnp.dot(
                poly[other], poly[half], precision=HIGHEST, preferred_element_type=jnp.float32
            )
            - poly[other - half]
        )
    for k in range(MOMENTS):
        poly_ref[k] = poly[k]


def project_kernel(mask_ref, left_ref, measured_ref, out_ref, staged, sems):
    _, _, views, depth, step, lanes = staged.shape
    columns = out_ref.shape[0]
    steps = columns // step

    def copy(i, side):
        start = pl.multiple_of(i * step + side * columns, step)
        return pltpu.make_async_copy(
            measured_ref.at[:, :, pl.ds(start, step), :],
            staged.at[i % 2, side],
            sems.at[i % 2, side],
        )

    for side in range(2):
        copy(0, side).start()
    half = tissue_half(mask_ref, lax.axis_index("gz"))
    here = tissue_lanes((depth, lanes), half)
    flat = staged.reshape(2 * 2 * views * depth * step, lanes)

    @pl.loop(0, steps)
    def _(i):
        @pl.when(i + 1 < steps)
        def _():
            for side in range(2):
                copy(i + 1, side).start()

        for side in range(2):
            copy(i, side).wait()

        def read(side, v, x):
            start = (((i % 2) * 2 + side) * views + v) * (depth * step) + x
            return flat[pl.ds(start, depth, stride=step), :]

        def packed(v, x):
            return jnp.where(here, read(0, v, x), pltpu.roll(read(1, v, x), lanes // 2, 1))

        for x in range(0, step, 2):
            parts = []
            for v in range(views):
                parts.append(
                    right_operand(jnp.concatenate([packed(v, x), packed(v, x + 1)], axis=1))
                )
            result = product(left_ref[...], jnp.concatenate(parts, axis=0))
            out_ref[i * step + x] = result[:, :lanes]
            out_ref[i * step + x + 1] = result[:, lanes:]


def residual_kernel(gram_ref, poly_ref, projected_ref, *refs):
    count = len(refs) - 3
    chunks, (residual_ref, moments_ref, square_ref) = refs[:count], refs[count:]
    columns, depth, lanes = projected_ref.shape
    slab = depth // count
    square_ref[...] = jnp.zeros_like(square_ref)

    def field(x):
        return jnp.concatenate([ref[x * slab : (x + 1) * slab, :] for ref in chunks], axis=0)

    for pair in range(columns // 2):
        x = 2 * pair
        image = product(
            gram_ref[...], right_operand(jnp.concatenate([field(x), field(x + 1)], axis=1))
        )
        start = jnp.concatenate([projected_ref[x], projected_ref[x + 1]], axis=1)
        both = right_operand(start - image)
        residual_ref[pair] = both
        square_ref[...] += lax.dot_general(
            both, both, (((1,), (1,)), ((), ())), preferred_element_type=jnp.float32
        )

    square = square_ref[...]
    square = (square[:depth, :depth] + square[depth:, depth:]) + (
        square[:depth, depth:] + square[depth:, :depth]
    )
    count = poly_ref.shape[0]
    sums = jnp.concatenate(
        [jnp.sum(square * poly_ref[k], axis=0, keepdims=True) for k in range(count)], axis=0
    )
    sums = jnp.sum(sums, axis=1, keepdims=True)
    lane = lax.broadcasted_iota(jnp.int32, (count, lanes), 1)
    order = lax.broadcasted_iota(jnp.int32, (count, lanes), 0)
    row = jnp.sum(jnp.where(lane == order, sums, 0.0), axis=0, keepdims=True)
    moments_ref[...] = jnp.broadcast_to(row, moments_ref.shape)


def conjugate(moments, centre, radius):
    def inner(p, q):
        total = None
        for i, a in enumerate(p):
            for j, b in enumerate(q):
                term = a * b * (0.5 * (moments[i + j] + moments[abs(i - j)]))
                total = term if total is None else total + term
        return total

    def operate(p):
        image = [centre * a for a in p] + [None]

        def put(i, value):
            image[i] = value if image[i] is None else image[i] + value

        for j, a in enumerate(p):
            if j == 0:
                put(1, radius * a)
            else:
                put(j + 1, 0.5 * radius * a)
                put(j - 1, 0.5 * radius * a)
        return image

    one = jnp.ones_like(moments[0])
    residual, direction = [one], [one]
    solved = []
    norm_now = moments[0]
    for iteration in range(ITERS):
        image = operate(direction)
        step_size = norm_now / inner(direction, image)
        solved = [s + step_size * d for s, d in zip(solved, direction)] + [
            step_size * d for d in direction[len(solved) :]
        ]
        if iteration == ITERS - 1:
            break
        residual = [r - step_size * i for r, i in zip(residual, image)] + [
            -step_size * i for i in image[len(residual) :]
        ]
        norm_next = inner(residual, residual)
        ratio = norm_next / norm_now
        direction = [r + ratio * d for r, d in zip(residual, direction)] + residual[len(direction) :]
        norm_now = norm_next
    return solved


def correct_kernel(top_ref, moments_ref, poly_ref, residual_ref, *refs):
    count = len(refs) - 2
    out_refs, (matrix_ref, left_ref) = refs[:count], refs[count:]
    depth = matrix_ref.shape[0]
    slab = depth // count
    pairs, _, lanes = residual_ref.shape
    lanes = lanes // 2
    me = lax.axis_index("gz")
    row = jnp.sum(moments_ref[...], axis=0, keepdims=True)
    lane = lax.broadcasted_iota(jnp.int32, row.shape, 1)
    moments = [
        jnp.sum(jnp.where(lane == k, row, 0.0), axis=1, keepdims=True) for k in range(MOMENTS)
    ]
    radius = 0.5 * top_ref[:1, :1]
    coefficients = conjugate(moments, damping + radius, radius)
    matrix = coefficients[0] * poly_ref[0]
    for k in range(1, ITERS):
        matrix = matrix + coefficients[k] * poly_ref[k]
    matrix_ref[...] = matrix
    left_ref[...] = left_operand(
        jnp.concatenate(
            [
                matrix_ref[pl.ds(pl.multiple_of(receiver(me, slot) * slab, slab), slab), :]
                for slot in slots(count)
            ],
            axis=0,
        )
    )
    for pair in range(pairs):
        result = product(left_ref[...], residual_ref[pair])
        for k in range(count):
            rows = result[slab * k : slab * (k + 1)]
            for side in range(2):
                start = (2 * pair + side) * slab
                out_refs[k][start : start + slab, :] = rows[:, lanes * side : lanes * (side + 1)]


def unpack_kernel(group, mask_ref, init_ref, *refs):
    count = len(group)
    chunks, (out_ref, staged, sems) = refs[:count], refs[-3:]
    _, slab, width, lanes = staged.shape
    columns = width // 2
    me = lax.axis_index("gz")
    flags = mask_ref[...]
    block = lax.broadcasted_iota(jnp.int32, flags.shape, 1)
    region = lax.broadcasted_iota(jnp.int32, flags.shape, 0)
    lane = lax.broadcasted_iota(jnp.int32, (columns, lanes), 1)
    stores = []
    for n, slot in enumerate(group):
        tile = sender(me, slot)
        start = pl.multiple_of(tile * width, width)
        chosen = (region == tile) & (block == 2 * lax.axis_index("gy") + 1)
        half = jnp.max(jnp.where(chosen, flags, 0), keepdims=True)
        here = (lane // (lanes // 2)) == half
        for z in range(slab):
            change = chunks[n][pl.ds(z, columns, stride=slab), :]
            staged[n, z, :columns, :] = init_ref[z, pl.ds(start, columns), :] + jnp.where(
                here, change, 0.0
            )
            staged[n, z, columns:, :] = init_ref[
                z, pl.ds(pl.multiple_of(start + columns, columns), columns), :
            ] + pltpu.roll(jnp.where(here, 0.0, change), lanes // 2, 1)
        stores.append(
            pltpu.make_async_copy(
                staged.at[n], out_ref.at[:, pl.ds(start, width), :], sems.at[n]
            )
        )
        stores[n].start()
    for store in stores:
        store.wait()


SMEM = pl.BlockSpec(memory_space=pltpu.SMEM)
VMEM = pl.BlockSpec(memory_space=pltpu.VMEM)
HBM = pl.BlockSpec(memory_space=pltpu.HBM)
ANY = pl.BlockSpec(memory_space=pl.ANY)


def cost(flops, read, transcendentals=0):
    return pl.CostEstimate(
        flops=int(flops), bytes_accessed=int(read), transcendentals=transcendentals
    )


def local(init, measured, mask, kernel_index, kernels):
    tiles, rows = lax.axis_size("gz"), lax.axis_size("gy")
    slab, _, lanes = init.shape
    views, depth, width, _ = measured.shape
    columns = width // 2
    f32, bf16 = jnp.float32, jnp.bfloat16
    shape = jax.ShapeDtypeStruct
    chunk = shape((columns * slab, lanes), f32)

    plan = slots(tiles)

    def exchange(blocks):
        arrived = list(blocks)
        for n in range(1, tiles):
            block = blocks[n]
            if n > IN_FLIGHT:
                before = n - IN_FLIGHT
                block, arrived[before] = lax.optimization_barrier((block, arrived[before]))
            route = [(j, j ^ plan[n][j % 2]) for j in range(tiles)]
            arrived[n] = lax.ppermute(block, "gz", route)
        return arrived

    packed = []
    for targets in (plan[1:4], [plan[0]] + plan[4:]):
        size = len(targets)
        packed += pl.pallas_call(
            functools.partial(pack_kernel, targets),
            name="pack_blocks",
            out_shape=[chunk] * size,
            in_specs=[HBM, HBM],
            out_specs=[VMEM] * size,
            scratch_shapes=[
                pltpu.VMEM((size, slab, width, lanes), f32),
                pltpu.SMEM(mask.shape, jnp.int32),
                pltpu.SemaphoreType.DMA((size,)),
                pltpu.SemaphoreType.DMA,
            ],
            compiler_params=pltpu.CompilerParams(vmem_limit_bytes=60 * MIB),
            cost_estimate=cost(init.size, 6 * init.size * size // tiles),
        )(mask, init)
    fields = exchange([packed[3]] + packed[:3] + packed[4:])

    poly_shape = shape((MOMENTS, depth, depth), f32)
    left, gram, poly, top = pl.pallas_call(
        tables_kernel,
        name="blur_tables",
        out_shape=[
            shape((2 * depth, 2 * views * depth), bf16),
            shape((2 * depth, 2 * depth), bf16),
            poly_shape,
            shape((8, lanes), f32),
        ],
        in_specs=[SMEM, VMEM],
        out_specs=[VMEM] * 4,
        scratch_shapes=[
            pltpu.VMEM((kernels.shape[0], depth), f32),
            pltpu.VMEM((kernels.shape[0], depth), f32),
            pltpu.VMEM((views * depth, depth), f32),
            pltpu.VMEM((depth, depth), f32),
        ],
        compiler_params=pltpu.CompilerParams(vmem_limit_bytes=8 * MIB),
        cost_estimate=cost(12 * 20 * depth**3, 4 * MIB),
    )(kernel_index, kernels)

    step = 8
    projected = pl.pallas_call(
        project_kernel,
        name="project_views",
        out_shape=shape((columns, depth, lanes), f32),
        in_specs=[SMEM, VMEM, HBM],
        out_specs=VMEM,
        scratch_shapes=[
            pltpu.VMEM((2, 2, views, depth, step, lanes), f32),
            pltpu.SemaphoreType.DMA((2, 2)),
        ],
        compiler_params=pltpu.CompilerParams(vmem_limit_bytes=48 * MIB),
        cost_estimate=cost(8 * views * depth * depth * columns * lanes, 4 * measured.size),
    )(mask, left, measured)

    everyone = tiles * rows
    pairs = columns // 2
    residual, moments = pl.pallas_call(
        residual_kernel,
        name="first_residual",
        out_shape=[
            shape((pairs, 2 * depth, 2 * lanes), bf16),
            shape((everyone, lanes), f32),
        ],
        in_specs=[VMEM] * (3 + tiles),
        out_specs=[VMEM] * 2,
        scratch_shapes=[pltpu.VMEM((2 * depth, 2 * depth), f32)],
        compiler_params=pltpu.CompilerParams(vmem_limit_bytes=16 * MIB),
        cost_estimate=cost(
            16 * depth * depth * columns * lanes, 12 * depth * columns * lanes
        ),
    )(gram, poly, projected, *fields)

    moments = lax.all_to_all(moments, ("gz", "gy"), split_axis=0, concat_axis=0, tiled=True)

    changes = pl.pallas_call(
        correct_kernel,
        name="correction",
        out_shape=[chunk] * tiles,
        in_specs=[VMEM] * 4,
        out_specs=[VMEM] * tiles,
        scratch_shapes=[
            pltpu.VMEM((depth, depth), f32),
            pltpu.VMEM((2 * depth, 2 * depth), bf16),
        ],
        compiler_params=pltpu.CompilerParams(vmem_limit_bytes=16 * MIB),
        cost_estimate=cost(8 * depth * depth * columns * lanes, 8 * depth * columns * lanes),
    )(top, moments, poly, residual)
    changes = exchange(changes)

    solved = None
    cut = [0, tiles // 2, tiles - 2, tiles]
    for first, last in zip(cut, cut[1:]):
        size = last - first
        earlier = [] if solved is None else [solved]
        solved = pl.pallas_call(
            functools.partial(unpack_kernel, plan[first:last]),
            name="add_correction",
            out_shape=shape(init.shape, f32),
            in_specs=[VMEM] * (2 + size) + [ANY] * len(earlier),
            out_specs=ANY,
            input_output_aliases={2 + size: 0} if earlier else {},
            scratch_shapes=[
                pltpu.VMEM((size, slab, width, lanes), f32),
                pltpu.SemaphoreType.DMA((size,)),
            ],
            compiler_params=pltpu.CompilerParams(vmem_limit_bytes=16 * MIB),
            cost_estimate=cost(init.size // 4, 5 * init.size * size // tiles),
        )(mask, init, *changes[first:last], *earlier)
    return solved


def solution(mesh):
    return jax.shard_map(
        local,
        mesh=mesh,
        in_specs=(P("gz", None, "gy"), P(None, None, "gz", "gy"), P(), P(), P()),
        out_specs=P("gz", None, "gy"),
        check_vma=False,
    )
```

```python
import functools

import jax
import jax.numpy as jnp
from jax import lax
from jax.experimental import pallas as pl
from jax.experimental.pallas import tpu as pltpu
from jax.sharding import PartitionSpec as P

ITERS = 4
MOMENTS = 2 * ITERS

HIGHEST = lax.Precision.HIGHEST
damping = 1.0
MIB = 1 << 20
IN_FLIGHT = 5


def split(x):
    high = x.astype(jnp.bfloat16)
    return high, (x - high.astype(jnp.float32)).astype(jnp.bfloat16)


def left_operand(matrix):
    high, low = split(matrix)
    return jnp.concatenate(
        [jnp.concatenate([high, high], axis=1), jnp.concatenate([low, low], axis=1)], axis=0
    )


def right_operand(matrix):
    return jnp.concatenate(split(matrix), axis=0)


def product(left, right):
    both = jnp.dot(left, right, preferred_element_type=jnp.float32)
    rows = both.shape[0] // 2
    return both[:rows] + both[rows:]


def slots(tiles):
    high = (tiles.bit_length() - 2) // 2

    def swapped(k):
        across = k >> 1
        if 4 ** high * 2 != tiles:
            return k
        return ((((across & (2**high - 1)) << high) | (across >> high)) << 1) | (k & 1)

    same, other = list(range(2, tiles, 2)), list(range(3, tiles, 2))
    order = [0, 1] + same + other
    return [(k, swapped(k)) for k in order]


def receiver(me, slot):
    even, odd = slot
    return jnp.bitwise_xor(me, even if even == odd else jnp.where(me % 2 == 0, even, odd))


def sender(me, slot):
    even, odd = slot
    return receiver(me, slot if even % 2 == 0 else (odd, even))


def tissue_half(mask_ref, tile):
    return mask_ref[tile, 2 * lax.axis_index("gy") + 1]


def tissue_lanes(shape, half):
    lane = lax.broadcasted_iota(jnp.int32, shape, len(shape) - 1)
    return (lane >= shape[-1] // 2) == (half == 1)


def pack_kernel(targets, mask_ref, init_ref, *refs):
    count = len(targets)
    out_refs, (staged, flags, sems, flag_sem) = refs[:count], refs[count:]
    _, slab, width, lanes = staged.shape
    columns = width // 2
    me = lax.axis_index("gz")

    def copy(n):
        start = pl.multiple_of(receiver(me, targets[n]) * width, width)
        return pltpu.make_async_copy(
            init_ref.at[:, pl.ds(start, width), :], staged.at[n], sems.at[n]
        )

    flag_copy = pltpu.make_async_copy(mask_ref, flags, flag_sem)
    flag_copy.start()
    for n in range(count):
        copy(n).start()
    flag_copy.wait()
    for n in range(count):
        copy(n).wait()
        half = tissue_half(flags, receiver(me, targets[n]))
        here = tissue_lanes((columns, lanes), half)
        for z in range(slab):
            first = staged[n, z, :columns, :]
            second = pltpu.roll(staged[n, z, columns:, :], lanes // 2, 1)
            out_refs[n][pl.ds(z, columns, stride=slab), :] = jnp.where(here, first, second)


def tables_kernel(
    index_ref, kernels_ref, left_ref, gram_ref, poly_ref, top_ref, bank, boxes, blur, square
):
    views, zbands, xbands = index_ref.shape
    taps = kernels_ref.shape[1]
    depth = poly_ref.shape[-1]
    zwidth = depth // zbands
    reach = taps // 2
    me = lax.axis_index("gz")

    def pick(ref, v, zband, xband):
        return ref[pl.ds(index_ref[v, zband, xband], 1), :]

    bank[...] = jnp.zeros_like(bank)
    bank[:, :taps] = kernels_ref[...]
    rows = bank[...]
    box = rows
    for r in range(1, zwidth):
        box = box + pltpu.roll(rows, r, 1)
    boxes[...] = box * jnp.sum(rows, axis=1, keepdims=True)

    def row_sums(xband, largest):
        total = jnp.zeros((1, depth), jnp.float32)
        for zband in range(zbands):
            part = pick(boxes, 0, zband, xband)
            for v in range(1, views):
                part = part + pick(boxes, v, zband, xband)
            total = total + pltpu.roll(part, (zband * zwidth - reach) % depth, 1)
        return jnp.maximum(largest, total)

    largest = lax.fori_loop(0, xbands, row_sums, jnp.zeros((1, depth), jnp.float32))
    top = jnp.max(largest, axis=1, keepdims=True)
    top_ref[...] = jnp.broadcast_to(top, top_ref.shape)

    z = lax.broadcasted_iota(jnp.int32, (zwidth, depth), 0)
    w = lax.broadcasted_iota(jnp.int32, (zwidth, depth), 1)
    for v in range(views):
        for zband in range(zbands):
            first = zband * zwidth
            row = jnp.broadcast_to(pick(bank, v, zband, me), (zwidth, depth))
            row = pltpu.roll(row, (first - reach) % depth, 1, stride=1, stride_axis=0)
            blur[v * depth + first : v * depth + first + zwidth, :] = jnp.where(
                jnp.abs(w - z - first) <= reach, row, 0.0
            )
    across = blur[...].T
    for v in range(views):
        left_ref[:, 2 * depth * v : 2 * depth * (v + 1)] = left_operand(
            across[:, depth * v : depth * (v + 1)]
        )
    gram = jnp.dot(across, blur[...], precision=HIGHEST, preferred_element_type=jnp.float32)
    square[...] = gram
    tiles = xbands
    slab = depth // tiles
    swapped = jnp.concatenate(
        [
            square[pl.ds(pl.multiple_of(sender(me, slot) * slab, slab), slab), :]
            for slot in slots(tiles)
        ],
        axis=0,
    )
    gram_ref[...] = left_operand(swapped.T)

    eye = jnp.where(
        lax.broadcasted_iota(jnp.int32, (depth, depth), 0)
        == lax.broadcasted_iota(jnp.int32, (depth, depth), 1),
        1.0,
        0.0,
    )
    poly = [eye, gram * (2.0 / top) - eye]
    for k in range(2, MOMENTS):
        half = k // 2
        other = k - half
        poly.append(
            2.0
            * jnp.dot(
                poly[other], poly[half], precision=HIGHEST, preferred_element_type=jnp.float32
            )
            - poly[other - half]
        )
    for k in range(MOMENTS):
        poly_ref[k] = poly[k]


def project_kernel(mask_ref, left_ref, measured_ref, out_ref, staged, sems):
    _, _, views, depth, step, lanes = staged.shape
    columns = out_ref.shape[0]
    steps = columns // step

    def copy(i, side):
        start = pl.multiple_of(i * step + side * columns, step)
        return pltpu.make_async_copy(
            measured_ref.at[:, :, pl.ds(start, step), :],
            staged.at[i % 2, side],
            sems.at[i % 2, side],
        )

    for side in range(2):
        copy(0, side).start()
    half = tissue_half(mask_ref, lax.axis_index("gz"))
    here = tissue_lanes((depth, lanes), half)
    flat = staged.reshape(2 * 2 * views * depth * step, lanes)

    @pl.loop(0, steps)
    def _(i):
        @pl.when(i + 1 < steps)
        def _():
            for side in range(2):
                copy(i + 1, side).start()

        for side in range(2):
            copy(i, side).wait()

        def read(side, v, x):
            start = (((i % 2) * 2 + side) * views + v) * (depth * step) + x
            return flat[pl.ds(start, depth, stride=step), :]

        def packed(v, x):
            return jnp.where(here, read(0, v, x), pltpu.roll(read(1, v, x), lanes // 2, 1))

        for x in range(0, step, 2):
            parts = []
            for v in range(views):
                parts.append(
                    right_operand(jnp.concatenate([packed(v, x), packed(v, x + 1)], axis=1))
                )
            result = product(left_ref[...], jnp.concatenate(parts, axis=0))
            out_ref[i * step + x] = result[:, :lanes]
            out_ref[i * step + x + 1] = result[:, lanes:]


def residual_kernel(gram_ref, poly_ref, projected_ref, *refs):
    count = len(refs) - 3
    chunks, (residual_ref, moments_ref, square_ref) = refs[:count], refs[count:]
    columns, depth, lanes = projected_ref.shape
    slab = depth // count
    square_ref[...] = jnp.zeros_like(square_ref)

    def field(x):
        return jnp.concatenate([ref[x * slab : (x + 1) * slab, :] for ref in chunks], axis=0)

    for pair in range(columns // 2):
        x = 2 * pair
        image = product(
            gram_ref[...], right_operand(jnp.concatenate([field(x), field(x + 1)], axis=1))
        )
        start = jnp.concatenate([projected_ref[x], projected_ref[x + 1]], axis=1)
        both = right_operand(start - image)
        residual_ref[pair] = both
        square_ref[...] += lax.dot_general(
            both, both, (((1,), (1,)), ((), ())), preferred_element_type=jnp.float32
        )

    square = square_ref[...]
    square = (square[:depth, :depth] + square[depth:, depth:]) + (
        square[:depth, depth:] + square[depth:, :depth]
    )
    count = poly_ref.shape[0]
    sums = jnp.concatenate(
        [jnp.sum(square * poly_ref[k], axis=0, keepdims=True) for k in range(count)], axis=0
    )
    sums = jnp.sum(sums, axis=1, keepdims=True)
    lane = lax.broadcasted_iota(jnp.int32, (count, lanes), 1)
    order = lax.broadcasted_iota(jnp.int32, (count, lanes), 0)
    row = jnp.sum(jnp.where(lane == order, sums, 0.0), axis=0, keepdims=True)
    moments_ref[...] = jnp.broadcast_to(row, moments_ref.shape)


def conjugate(moments, centre, radius):
    def inner(p, q):
        total = None
        for i, a in enumerate(p):
            for j, b in enumerate(q):
                term = a * b * (0.5 * (moments[i + j] + moments[abs(i - j)]))
                total = term if total is None else total + term
        return total

    def operate(p):
        image = [centre * a for a in p] + [None]

        def put(i, value):
            image[i] = value if image[i] is None else image[i] + value

        for j, a in enumerate(p):
            if j == 0:
                put(1, radius * a)
            else:
                put(j + 1, 0.5 * radius * a)
                put(j - 1, 0.5 * radius * a)
        return image

    one = jnp.ones_like(moments[0])
    residual, direction = [one], [one]
    solved = []
    norm_now = moments[0]
    for iteration in range(ITERS):
        image = operate(direction)
        step_size = norm_now / inner(direction, image)
        solved = [s + step_size * d for s, d in zip(solved, direction)] + [
            step_size * d for d in direction[len(solved) :]
        ]
        if iteration == ITERS - 1:
            break
        residual = [r - step_size * i for r, i in zip(residual, image)] + [
            -step_size * i for i in image[len(residual) :]
        ]
        norm_next = inner(residual, residual)
        ratio = norm_next / norm_now
        direction = [r + ratio * d for r, d in zip(residual, direction)] + residual[len(direction) :]
        norm_now = norm_next
    return solved


def correct_kernel(top_ref, moments_ref, poly_ref, residual_ref, *refs):
    count = len(refs) - 2
    out_refs, (matrix_ref, left_ref) = refs[:count], refs[count:]
    depth = matrix_ref.shape[0]
    slab = depth // count
    pairs, _, lanes = residual_ref.shape
    lanes = lanes // 2
    me = lax.axis_index("gz")
    row = jnp.sum(moments_ref[...], axis=0, keepdims=True)
    lane = lax.broadcasted_iota(jnp.int32, row.shape, 1)
    moments = [
        jnp.sum(jnp.where(lane == k, row, 0.0), axis=1, keepdims=True) for k in range(MOMENTS)
    ]
    radius = 0.5 * top_ref[:1, :1]
    coefficients = conjugate(moments, damping + radius, radius)
    matrix = coefficients[0] * poly_ref[0]
    for k in range(1, ITERS):
        matrix = matrix + coefficients[k] * poly_ref[k]
    matrix_ref[...] = matrix
    left_ref[...] = left_operand(
        jnp.concatenate(
            [
                matrix_ref[pl.ds(pl.multiple_of(receiver(me, slot) * slab, slab), slab), :]
                for slot in slots(count)
            ],
            axis=0,
        )
    )
    for pair in range(pairs):
        result = product(left_ref[...], residual_ref[pair])
        for k in range(count):
            rows = result[slab * k : slab * (k + 1)]
            for side in range(2):
                start = (2 * pair + side) * slab
                out_refs[k][start : start + slab, :] = rows[:, lanes * side : lanes * (side + 1)]


def unpack_kernel(group, mask_ref, init_ref, *refs):
    count = len(group)
    chunks, (out_ref, staged, sems) = refs[:count], refs[-3:]
    _, slab, width, lanes = staged.shape
    columns = width // 2
    me = lax.axis_index("gz")
    flags = mask_ref[...]
    block = lax.broadcasted_iota(jnp.int32, flags.shape, 1)
    region = lax.broadcasted_iota(jnp.int32, flags.shape, 0)
    lane = lax.broadcasted_iota(jnp.int32, (columns, lanes), 1)
    stores = []
    for n, slot in enumerate(group):
        tile = sender(me, slot)
        start = pl.multiple_of(tile * width, width)
        chosen = (region == tile) & (block == 2 * lax.axis_index("gy") + 1)
        half = jnp.max(jnp.where(chosen, flags, 0), keepdims=True)
        here = (lane // (lanes // 2)) == half
        for z in range(slab):
            change = chunks[n][pl.ds(z, columns, stride=slab), :]
            staged[n, z, :columns, :] = init_ref[z, pl.ds(start, columns), :] + jnp.where(
                here, change, 0.0
            )
            staged[n, z, columns:, :] = init_ref[
                z, pl.ds(pl.multiple_of(start + columns, columns), columns), :
            ] + pltpu.roll(jnp.where(here, 0.0, change), lanes // 2, 1)
        stores.append(
            pltpu.make_async_copy(
                staged.at[n], out_ref.at[:, pl.ds(start, width), :], sems.at[n]
            )
        )
        stores[n].start()
    for store in stores:
        store.wait()


SMEM = pl.BlockSpec(memory_space=pltpu.SMEM)
VMEM = pl.BlockSpec(memory_space=pltpu.VMEM)
HBM = pl.BlockSpec(memory_space=pltpu.HBM)
ANY = pl.BlockSpec(memory_space=pl.ANY)


def cost(flops, read, transcendentals=0):
    return pl.CostEstimate(
        flops=int(flops), bytes_accessed=int(read), transcendentals=transcendentals
    )


def local(init, measured, mask, kernel_index, kernels):
    tiles, rows = lax.axis_size("gz"), lax.axis_size("gy")
    slab, _, lanes = init.shape
    views, depth, width, _ = measured.shape
    columns = width // 2
    f32, bf16 = jnp.float32, jnp.bfloat16
    shape = jax.ShapeDtypeStruct
    chunk = shape((columns * slab, lanes), f32)

    plan = slots(tiles)

    def exchange(blocks):
        arrived = list(blocks)
        for n in range(1, tiles):
            block = blocks[n]
            if n > IN_FLIGHT:
                before = n - IN_FLIGHT
                block, arrived[before] = lax.optimization_barrier((block, arrived[before]))
            route = [(j, j ^ plan[n][j % 2]) for j in range(tiles)]
            arrived[n] = lax.ppermute(block, "gz", route)
        return arrived

    init_hbm, measured, mask_hbm = (
        pltpu.with_memory_space_constraint(x, pltpu.HBM) for x in (init, measured, mask)
    )
    packed = []
    for targets in (plan[1:4], [plan[0]] + plan[4:]):
        size = len(targets)
        packed += pl.pallas_call(
            functools.partial(pack_kernel, targets),
            name="pack_blocks",
            out_shape=[pltpu.VMEM(chunk.shape, f32)] * size,
            in_specs=[HBM, HBM],
            out_specs=[VMEM] * size,
            scratch_shapes=[
                pltpu.VMEM((size, slab, width, lanes), f32),
                pltpu.SMEM(mask.shape, jnp.int32),
                pltpu.SemaphoreType.DMA((size,)),
                pltpu.SemaphoreType.DMA,
            ],
            compiler_params=pltpu.CompilerParams(vmem_limit_bytes=16 * MIB),
            cost_estimate=cost(init.size, 6 * init.size * size // tiles),
        )(mask_hbm, init_hbm)
    fields = exchange([packed[3]] + packed[:3] + packed[4:])

    poly_shape = shape((MOMENTS, depth, depth), f32)
    left, gram, poly, top = pl.pallas_call(
        tables_kernel,
        name="blur_tables",
        out_shape=[
            shape((2 * depth, 2 * views * depth), bf16),
            shape((2 * depth, 2 * depth), bf16),
            poly_shape,
            shape((8, lanes), f32),
        ],
        in_specs=[SMEM, VMEM],
        out_specs=[VMEM] * 4,
        scratch_shapes=[
            pltpu.VMEM((kernels.shape[0], depth), f32),
            pltpu.VMEM((kernels.shape[0], depth), f32),
            pltpu.VMEM((views * depth, depth), f32),
            pltpu.VMEM((depth, depth), f32),
        ],
        compiler_params=pltpu.CompilerParams(vmem_limit_bytes=8 * MIB),
        cost_estimate=cost(12 * 20 * depth**3, 4 * MIB),
    )(kernel_index, kernels)

    step = 8
    projected = pl.pallas_call(
        project_kernel,
        name="project_views",
        out_shape=shape((columns, depth, lanes), f32),
        in_specs=[SMEM, VMEM, HBM],
        out_specs=VMEM,
        scratch_shapes=[
            pltpu.VMEM((2, 2, views, depth, step, lanes), f32),
            pltpu.SemaphoreType.DMA((2, 2)),
        ],
        compiler_params=pltpu.CompilerParams(vmem_limit_bytes=16 * MIB),
        cost_estimate=cost(8 * views * depth * depth * columns * lanes, 4 * measured.size),
    )(mask, left, measured)

    everyone = tiles * rows
    pairs = columns // 2
    residual, moments = pl.pallas_call(
        residual_kernel,
        name="first_residual",
        out_shape=[
            shape((pairs, 2 * depth, 2 * lanes), bf16),
            shape((everyone, lanes), f32),
        ],
        in_specs=[VMEM] * (3 + tiles),
        out_specs=[VMEM] * 2,
        scratch_shapes=[pltpu.VMEM((2 * depth, 2 * depth), f32)],
        compiler_params=pltpu.CompilerParams(vmem_limit_bytes=16 * MIB),
        cost_estimate=cost(
            16 * depth * depth * columns * lanes, 12 * depth * columns * lanes
        ),
    )(gram, poly, projected, *fields)

    moments = lax.all_to_all(moments, ("gz", "gy"), split_axis=0, concat_axis=0, tiled=True)

    changes = pl.pallas_call(
        correct_kernel,
        name="correction",
        out_shape=[chunk] * tiles,
        in_specs=[VMEM] * 4,
        out_specs=[VMEM] * tiles,
        scratch_shapes=[
            pltpu.VMEM((depth, depth), f32),
            pltpu.VMEM((2 * depth, 2 * depth), bf16),
        ],
        compiler_params=pltpu.CompilerParams(vmem_limit_bytes=16 * MIB),
        cost_estimate=cost(8 * depth * depth * columns * lanes, 8 * depth * columns * lanes),
    )(top, moments, poly, residual)
    changes = exchange(changes)

    solved = None
    cut = [0, tiles // 2, tiles - 3, tiles - 1, tiles]
    for first, last in zip(cut, cut[1:]):
        size = last - first
        earlier = [] if solved is None else [solved]
        solved = pl.pallas_call(
            functools.partial(unpack_kernel, plan[first:last]),
            name="add_correction",
            out_shape=shape(init.shape, f32),
            in_specs=[VMEM] * (2 + size) + [ANY] * len(earlier),
            out_specs=ANY,
            input_output_aliases={2 + size: 0} if earlier else {},
            scratch_shapes=[
                pltpu.VMEM((size, slab, width, lanes), f32),
                pltpu.SemaphoreType.DMA((size,)),
            ],
            compiler_params=pltpu.CompilerParams(vmem_limit_bytes=16 * MIB),
            cost_estimate=cost(init.size // 4, 5 * init.size * size // tiles),
        )(mask, init, *changes[first:last], *earlier)
    return solved


def solution(mesh):
    return jax.shard_map(
        local,
        mesh=mesh,
        in_specs=(P("gz", None, "gy"), P(None, None, "gz", "gy"), P(), P(), P()),
        out_specs=P("gz", None, "gy"),
        check_vma=False,
    )
```

```python
import functools

import jax
import jax.numpy as jnp
from jax import lax
from jax.experimental import pallas as pl
from jax.experimental.pallas import tpu as pltpu
from jax.sharding import PartitionSpec as P

ITERS = 4
MOMENTS = 2 * ITERS

HIGHEST = lax.Precision.HIGHEST
damping = 1.0
MIB = 1 << 20
IN_FLIGHT = 5
EARLY = 3


def split(x):
    high = x.astype(jnp.bfloat16)
    return high, (x - high.astype(jnp.float32)).astype(jnp.bfloat16)


def left_operand(matrix):
    high, low = split(matrix)
    return jnp.concatenate(
        [jnp.concatenate([high, high], axis=1), jnp.concatenate([low, low], axis=1)], axis=0
    )


def right_operand(matrix):
    return jnp.concatenate(split(matrix), axis=0)


def product(left, right):
    both = jnp.dot(left, right, preferred_element_type=jnp.float32)
    rows = both.shape[0] // 2
    return both[:rows] + both[rows:]


def slots(tiles):
    high = (tiles.bit_length() - 2) // 2

    def swapped(k):
        across = k >> 1
        if 4 ** high * 2 != tiles:
            return k
        return ((((across & (2**high - 1)) << high) | (across >> high)) << 1) | (k & 1)

    same, other = list(range(2, tiles, 2)), list(range(3, tiles, 2))
    order = [0] + same[:2] + [1] + same[2:] + other
    return [(k, swapped(k)) for k in order]


def receiver(me, slot):
    even, odd = slot
    return jnp.bitwise_xor(me, even if even == odd else jnp.where(me % 2 == 0, even, odd))


def sender(me, slot):
    even, odd = slot
    return receiver(me, slot if even % 2 == 0 else (odd, even))


def tissue_half(mask_ref, tile):
    return mask_ref[tile, 2 * lax.axis_index("gy") + 1]


def tissue_lanes(shape, half):
    lane = lax.broadcasted_iota(jnp.int32, shape, len(shape) - 1)
    return (lane >= shape[-1] // 2) == (half == 1)


def pack_kernel(targets, mask_ref, init_ref, *refs):
    count = len(targets)
    out_refs, (staged, flags, sems, flag_sem) = refs[:count], refs[count:]
    _, slab, width, lanes = staged.shape
    columns = width // 2
    me = lax.axis_index("gz")

    def copy(n):
        start = pl.multiple_of(receiver(me, targets[n]) * width, width)
        return pltpu.make_async_copy(
            init_ref.at[:, pl.ds(start, width), :], staged.at[n], sems.at[n]
        )

    flag_copy = pltpu.make_async_copy(mask_ref, flags, flag_sem)
    flag_copy.start()
    for n in range(count):
        copy(n).start()
    flag_copy.wait()
    for n in range(count):
        copy(n).wait()
        half = tissue_half(flags, receiver(me, targets[n]))
        here = tissue_lanes((columns, lanes), half)
        for z in range(slab):
            first = staged[n, z, :columns, :]
            second = pltpu.roll(staged[n, z, columns:, :], lanes // 2, 1)
            out_refs[n][pl.ds(z, columns, stride=slab), :] = jnp.where(here, first, second)


def tables_kernel(
    index_ref, kernels_ref, left_ref, gram_ref, poly_ref, top_ref, bank, boxes, blur, square
):
    views, zbands, xbands = index_ref.shape
    taps = kernels_ref.shape[1]
    depth = poly_ref.shape[-1]
    zwidth = depth // zbands
    reach = taps // 2
    me = lax.axis_index("gz")

    def pick(ref, v, zband, xband):
        return ref[pl.ds(index_ref[v, zband, xband], 1), :]

    bank[...] = jnp.zeros_like(bank)
    bank[:, :taps] = kernels_ref[...]
    rows = bank[...]
    box = rows
    for r in range(1, zwidth):
        box = box + pltpu.roll(rows, r, 1)
    boxes[...] = box * jnp.sum(rows, axis=1, keepdims=True)

    def row_sums(xband, largest):
        total = jnp.zeros((1, depth), jnp.float32)
        for zband in range(zbands):
            part = pick(boxes, 0, zband, xband)
            for v in range(1, views):
                part = part + pick(boxes, v, zband, xband)
            total = total + pltpu.roll(part, (zband * zwidth - reach) % depth, 1)
        return jnp.maximum(largest, total)

    largest = lax.fori_loop(0, xbands, row_sums, jnp.zeros((1, depth), jnp.float32))
    top = jnp.max(largest, axis=1, keepdims=True)
    top_ref[...] = jnp.broadcast_to(top, top_ref.shape)

    z = lax.broadcasted_iota(jnp.int32, (zwidth, depth), 0)
    w = lax.broadcasted_iota(jnp.int32, (zwidth, depth), 1)
    for v in range(views):
        for zband in range(zbands):
            first = zband * zwidth
            row = jnp.broadcast_to(pick(bank, v, zband, me), (zwidth, depth))
            row = pltpu.roll(row, (first - reach) % depth, 1, stride=1, stride_axis=0)
            blur[v * depth + first : v * depth + first + zwidth, :] = jnp.where(
                jnp.abs(w - z - first) <= reach, row, 0.0
            )
    across = blur[...].T
    for v in range(views):
        left_ref[:, 2 * depth * v : 2 * depth * (v + 1)] = left_operand(
            across[:, depth * v : depth * (v + 1)]
        )
    gram = jnp.dot(across, blur[...], precision=HIGHEST, preferred_element_type=jnp.float32)
    square[...] = gram
    tiles = xbands
    slab = depth // tiles
    swapped = jnp.concatenate(
        [
            square[pl.ds(pl.multiple_of(sender(me, slot) * slab, slab), slab), :]
            for slot in slots(tiles)
        ],
        axis=0,
    )
    gram_ref[...] = left_operand(swapped.T)

    eye = jnp.where(
        lax.broadcasted_iota(jnp.int32, (depth, depth), 0)
        == lax.broadcasted_iota(jnp.int32, (depth, depth), 1),
        1.0,
        0.0,
    )
    poly = [eye, gram * (2.0 / top) - eye]
    for k in range(2, MOMENTS):
        half = k // 2
        other = k - half
        poly.append(
            2.0
            * jnp.dot(
                poly[other], poly[half], precision=HIGHEST, preferred_element_type=jnp.float32
            )
            - poly[other - half]
        )
    for k in range(MOMENTS):
        poly_ref[k] = poly[k]


def project_kernel(mask_ref, left_ref, measured_ref, out_ref, staged, sems):
    _, _, views, depth, step, lanes = staged.shape
    columns = out_ref.shape[0]
    steps = columns // step

    def copy(i, side):
        start = pl.multiple_of(i * step + side * columns, step)
        return pltpu.make_async_copy(
            measured_ref.at[:, :, pl.ds(start, step), :],
            staged.at[i % 2, side],
            sems.at[i % 2, side],
        )

    for side in range(2):
        copy(0, side).start()
    half = tissue_half(mask_ref, lax.axis_index("gz"))
    here = tissue_lanes((depth, lanes), half)
    flat = staged.reshape(2 * 2 * views * depth * step, lanes)

    @pl.loop(0, steps)
    def _(i):
        @pl.when(i + 1 < steps)
        def _():
            for side in range(2):
                copy(i + 1, side).start()

        for side in range(2):
            copy(i, side).wait()

        def read(side, v, x):
            start = (((i % 2) * 2 + side) * views + v) * (depth * step) + x
            return flat[pl.ds(start, depth, stride=step), :]

        def packed(v, x):
            return jnp.where(here, read(0, v, x), pltpu.roll(read(1, v, x), lanes // 2, 1))

        for x in range(0, step, 2):
            parts = []
            for v in range(views):
                parts.append(
                    right_operand(jnp.concatenate([packed(v, x), packed(v, x + 1)], axis=1))
                )
            result = product(left_ref[...], jnp.concatenate(parts, axis=0))
            out_ref[i * step + x] = result[:, :lanes]
            out_ref[i * step + x + 1] = result[:, lanes:]


def residual_kernel(gram_ref, poly_ref, projected_ref, *refs):
    count = len(refs) - 3
    chunks, (residual_ref, moments_ref, square_ref) = refs[:count], refs[count:]
    columns, depth, lanes = projected_ref.shape
    slab = depth // count
    square_ref[...] = jnp.zeros_like(square_ref)

    def field(x):
        return jnp.concatenate([ref[x * slab : (x + 1) * slab, :] for ref in chunks], axis=0)

    for pair in range(columns // 2):
        x = 2 * pair
        image = product(
            gram_ref[...], right_operand(jnp.concatenate([field(x), field(x + 1)], axis=1))
        )
        start = jnp.concatenate([projected_ref[x], projected_ref[x + 1]], axis=1)
        both = right_operand(start - image)
        residual_ref[pair] = both
        square_ref[...] += lax.dot_general(
            both, both, (((1,), (1,)), ((), ())), preferred_element_type=jnp.float32
        )

    square = square_ref[...]
    square = (square[:depth, :depth] + square[depth:, depth:]) + (
        square[:depth, depth:] + square[depth:, :depth]
    )
    count = poly_ref.shape[0]
    sums = jnp.concatenate(
        [jnp.sum(square * poly_ref[k], axis=0, keepdims=True) for k in range(count)], axis=0
    )
    sums = jnp.sum(sums, axis=1, keepdims=True)
    lane = lax.broadcasted_iota(jnp.int32, (count, lanes), 1)
    order = lax.broadcasted_iota(jnp.int32, (count, lanes), 0)
    row = jnp.sum(jnp.where(lane == order, sums, 0.0), axis=0, keepdims=True)
    moments_ref[...] = jnp.broadcast_to(row, moments_ref.shape)


def conjugate(moments, centre, radius):
    def inner(p, q):
        total = None
        for i, a in enumerate(p):
            for j, b in enumerate(q):
                term = a * b * (0.5 * (moments[i + j] + moments[abs(i - j)]))
                total = term if total is None else total + term
        return total

    def operate(p):
        image = [centre * a for a in p] + [None]

        def put(i, value):
            image[i] = value if image[i] is None else image[i] + value

        for j, a in enumerate(p):
            if j == 0:
                put(1, radius * a)
            else:
                put(j + 1, 0.5 * radius * a)
                put(j - 1, 0.5 * radius * a)
        return image

    one = jnp.ones_like(moments[0])
    residual, direction = [one], [one]
    solved = []
    norm_now = moments[0]
    for iteration in range(ITERS):
        image = operate(direction)
        step_size = norm_now / inner(direction, image)
        solved = [s + step_size * d for s, d in zip(solved, direction)] + [
            step_size * d for d in direction[len(solved) :]
        ]
        if iteration == ITERS - 1:
            break
        residual = [r - step_size * i for r, i in zip(residual, image)] + [
            -step_size * i for i in image[len(residual) :]
        ]
        norm_next = inner(residual, residual)
        ratio = norm_next / norm_now
        direction = [r + ratio * d for r, d in zip(residual, direction)] + residual[len(direction) :]
        norm_now = norm_next
    return solved


def combine_kernel(top_ref, moments_ref, poly_ref, matrix_ref):
    row = jnp.sum(moments_ref[...], axis=0, keepdims=True)
    lane = lax.broadcasted_iota(jnp.int32, row.shape, 1)
    moments = [
        jnp.sum(jnp.where(lane == k, row, 0.0), axis=1, keepdims=True) for k in range(MOMENTS)
    ]
    radius = 0.5 * top_ref[:1, :1]
    coefficients = conjugate(moments, damping + radius, radius)
    matrix = coefficients[0] * poly_ref[0]
    for k in range(1, ITERS):
        matrix = matrix + coefficients[k] * poly_ref[k]
    matrix_ref[...] = matrix


def correct_blocks(group, slab, matrix_ref, residual_ref, out_refs, left_ref):
    pairs, _, lanes = residual_ref.shape
    lanes = lanes // 2
    me = lax.axis_index("gz")
    left_ref[...] = left_operand(
        jnp.concatenate(
            [
                matrix_ref[pl.ds(pl.multiple_of(receiver(me, slot) * slab, slab), slab), :]
                for slot in group
            ],
            axis=0,
        )
    )
    for pair in range(pairs):
        result = product(left_ref[...], residual_ref[pair])
        for k in range(len(group)):
            rows = result[slab * k : slab * (k + 1)]
            for side in range(2):
                start = (2 * pair + side) * slab
                out_refs[k][start : start + slab, :] = rows[:, lanes * side : lanes * (side + 1)]


def first_correct_kernel(group, top_ref, moments_ref, poly_ref, residual_ref, matrix_ref, *refs):
    combine_kernel(top_ref, moments_ref, poly_ref, matrix_ref)
    slab = refs[0].shape[0] // (2 * residual_ref.shape[0])
    correct_blocks(group, slab, matrix_ref, residual_ref, refs[:-1], refs[-1])


def correct_kernel(group, matrix_ref, residual_ref, *refs):
    slab = refs[0].shape[0] // (2 * residual_ref.shape[0])
    correct_blocks(group, slab, matrix_ref, residual_ref, refs[:-1], refs[-1])


def unpack_kernel(group, mask_ref, init_ref, *refs):
    count = len(group)
    chunks, (out_ref, staged, sems) = refs[:count], refs[-3:]
    _, slab, width, lanes = staged.shape
    columns = width // 2
    me = lax.axis_index("gz")
    flags = mask_ref[...]
    block = lax.broadcasted_iota(jnp.int32, flags.shape, 1)
    region = lax.broadcasted_iota(jnp.int32, flags.shape, 0)
    lane = lax.broadcasted_iota(jnp.int32, (columns, lanes), 1)
    pieces = sems.shape[1]
    piece = slab // pieces
    stores = []
    for n, slot in enumerate(group):
        tile = sender(me, slot)
        start = pl.multiple_of(tile * width, width)
        chosen = (region == tile) & (block == 2 * lax.axis_index("gy") + 1)
        half = jnp.max(jnp.where(chosen, flags, 0), keepdims=True)
        here = (lane // (lanes // 2)) == half
        for z in range(slab):
            change = chunks[n][pl.ds(z, columns, stride=slab), :]
            staged[n, z, :columns, :] = init_ref[z, pl.ds(start, columns), :] + jnp.where(
                here, change, 0.0
            )
            staged[n, z, columns:, :] = init_ref[
                z, pl.ds(pl.multiple_of(start + columns, columns), columns), :
            ] + pltpu.roll(jnp.where(here, 0.0, change), lanes // 2, 1)
            if (z + 1) % piece == 0:
                part = pl.ds(z + 1 - piece, piece)
                stores.append(
                    pltpu.make_async_copy(
                        staged.at[n, part],
                        out_ref.at[part, pl.ds(start, width), :],
                        sems.at[n, z // piece],
                    )
                )
                stores[-1].start()
    for store in stores:
        store.wait()


SMEM = pl.BlockSpec(memory_space=pltpu.SMEM)
VMEM = pl.BlockSpec(memory_space=pltpu.VMEM)
HBM = pl.BlockSpec(memory_space=pltpu.HBM)
ANY = pl.BlockSpec(memory_space=pl.ANY)


def cost(flops, read, transcendentals=0):
    return pl.CostEstimate(
        flops=int(flops), bytes_accessed=int(read), transcendentals=transcendentals
    )


def local(init, measured, mask, kernel_index, kernels):
    tiles, rows = lax.axis_size("gz"), lax.axis_size("gy")
    slab, _, lanes = init.shape
    views, depth, width, _ = measured.shape
    columns = width // 2
    f32, bf16 = jnp.float32, jnp.bfloat16
    shape = jax.ShapeDtypeStruct
    chunk = shape((columns * slab, lanes), f32)

    plan = slots(tiles)

    def exchange(blocks):
        arrived = list(blocks)
        for n in range(1, tiles):
            block = blocks[n]
            if n > IN_FLIGHT:
                before = n - IN_FLIGHT
                block, arrived[before] = lax.optimization_barrier((block, arrived[before]))
            route = [(j, j ^ plan[n][j % 2]) for j in range(tiles)]
            arrived[n] = lax.ppermute(block, "gz", route)
        return arrived

    init_hbm, measured, mask_hbm = (
        pltpu.with_memory_space_constraint(x, pltpu.HBM) for x in (init, measured, mask)
    )
    packed = []
    for targets in (plan[1:3], [plan[0]] + plan[3:]):
        size = len(targets)
        packed += pl.pallas_call(
            functools.partial(pack_kernel, targets),
            name="pack_blocks",
            out_shape=[pltpu.VMEM(chunk.shape, f32)] * size,
            in_specs=[HBM, HBM],
            out_specs=[VMEM] * size,
            scratch_shapes=[
                pltpu.VMEM((size, slab, width, lanes), f32),
                pltpu.SMEM(mask.shape, jnp.int32),
                pltpu.SemaphoreType.DMA((size,)),
                pltpu.SemaphoreType.DMA,
            ],
            compiler_params=pltpu.CompilerParams(vmem_limit_bytes=16 * MIB),
            cost_estimate=cost(init.size, 6 * init.size * size // tiles),
        )(mask_hbm, init_hbm)
    fields = exchange([packed[2]] + packed[:2] + packed[3:])

    poly_shape = shape((MOMENTS, depth, depth), f32)
    left, gram, poly, top = pl.pallas_call(
        tables_kernel,
        name="blur_tables",
        out_shape=[
            shape((2 * depth, 2 * views * depth), bf16),
            shape((2 * depth, 2 * depth), bf16),
            poly_shape,
            shape((8, lanes), f32),
        ],
        in_specs=[SMEM, VMEM],
        out_specs=[VMEM] * 4,
        scratch_shapes=[
            pltpu.VMEM((kernels.shape[0], depth), f32),
            pltpu.VMEM((kernels.shape[0], depth), f32),
            pltpu.VMEM((views * depth, depth), f32),
            pltpu.VMEM((depth, depth), f32),
        ],
        compiler_params=pltpu.CompilerParams(vmem_limit_bytes=8 * MIB),
        cost_estimate=cost(12 * 20 * depth**3, 4 * MIB),
    )(kernel_index, kernels)

    step = 8
    projected = pl.pallas_call(
        project_kernel,
        name="project_views",
        out_shape=shape((columns, depth, lanes), f32),
        in_specs=[SMEM, VMEM, HBM],
        out_specs=VMEM,
        scratch_shapes=[
            pltpu.VMEM((2, 2, views, depth, step, lanes), f32),
            pltpu.SemaphoreType.DMA((2, 2)),
        ],
        compiler_params=pltpu.CompilerParams(vmem_limit_bytes=16 * MIB),
        cost_estimate=cost(8 * views * depth * depth * columns * lanes, 4 * measured.size),
    )(mask, left, measured)

    everyone = tiles * rows
    pairs = columns // 2
    residual, moments = pl.pallas_call(
        residual_kernel,
        name="first_residual",
        out_shape=[
            shape((pairs, 2 * depth, 2 * lanes), bf16),
            shape((everyone, lanes), f32),
        ],
        in_specs=[VMEM] * (3 + tiles),
        out_specs=[VMEM] * 2,
        scratch_shapes=[pltpu.VMEM((2 * depth, 2 * depth), f32)],
        compiler_params=pltpu.CompilerParams(vmem_limit_bytes=16 * MIB),
        cost_estimate=cost(
            16 * depth * depth * columns * lanes, 12 * depth * columns * lanes
        ),
    )(gram, poly, projected, *fields)

    moments = lax.all_to_all(moments, ("gz", "gy"), split_axis=0, concat_axis=0, tiled=True)

    parameters = pltpu.CompilerParams(vmem_limit_bytes=16 * MIB)
    soon, later = plan[1:EARLY], plan[:1] + plan[EARLY:]
    matrix, *changes = pl.pallas_call(
        functools.partial(first_correct_kernel, soon),
        name="first_corrections",
        out_shape=[shape((depth, depth), f32)] + [chunk] * len(soon),
        in_specs=[VMEM] * 4,
        out_specs=[VMEM] * (1 + len(soon)),
        scratch_shapes=[pltpu.VMEM((2 * slab * len(soon), 2 * depth), bf16)],
        compiler_params=parameters,
        cost_estimate=cost(2 * depth * depth * columns * lanes, 2 * depth * columns * lanes),
    )(top, moments, poly, residual)
    others = pl.pallas_call(
        functools.partial(correct_kernel, later),
        name="corrections",
        out_shape=[chunk] * len(later),
        in_specs=[VMEM] * 2,
        out_specs=[VMEM] * len(later),
        scratch_shapes=[pltpu.VMEM((2 * slab * len(later), 2 * depth), bf16)],
        compiler_params=parameters,
        cost_estimate=cost(6 * depth * depth * columns * lanes, 6 * depth * columns * lanes),
    )(matrix, residual)
    changes = [others[0], *changes, *others[1:]]
    changes = exchange(changes)

    solved = None
    cut = [0, tiles // 2, tiles - 3, tiles - 1, tiles]
    for first, last in zip(cut, cut[1:]):
        size = last - first
        earlier = [] if solved is None else [solved]
        solved = pl.pallas_call(
            functools.partial(unpack_kernel, plan[first:last]),
            name="add_correction",
            out_shape=shape(init.shape, f32),
            in_specs=[VMEM] * (2 + size) + [ANY] * len(earlier),
            out_specs=ANY,
            input_output_aliases={2 + size: 0} if earlier else {},
            scratch_shapes=[
                pltpu.VMEM((size, slab, width, lanes), f32),
                pltpu.SemaphoreType.DMA((size, 4)),
            ],
            compiler_params=pltpu.CompilerParams(vmem_limit_bytes=16 * MIB),
            cost_estimate=cost(init.size // 4, 5 * init.size * size // tiles),
        )(mask, init, *changes[first:last], *earlier)
    return solved


def solution(mesh):
    return jax.shard_map(
        local,
        mesh=mesh,
        in_specs=(P("gz", None, "gy"), P(None, None, "gz", "gy"), P(), P(), P()),
        out_specs=P("gz", None, "gy"),
        check_vma=False,
    )
```
